128 devices in a mesh: expert: 8 (over x_lo, z), tensor: 16 (over x_hi, y, core).
Axes of the slice: x: 4 (x_hi: 2, x_lo: 2; x = x_hi * 2 + x_lo), y: 4, z: 4, core: 2. Of those that a mesh axis runs over, the one named last changes fastest.
Arguments:
- tokens: bfloat16 [1024, 7168], P(('expert', 'tensor')), may hold values from -6 to 6
- route_ids: int32 [1024, 2], P(('expert', 'tensor')), may hold values from 0 to 7, all different within a row; in each aligned block of 128 rows (0 to 127, 128 to 255, ...) at most 64 rows name the same one
- route_gain: int32 [1024, 2], P(('expert', 'tensor')), may hold values from 1 to 1023
- norm_gain: float32 [7168], replicated, may hold values from 0.1 to 1.9
- dense_gate: bfloat16 [7168, 4864], P(None, 'tensor'), may hold values from -0.0625 to 0.0625
- dense_up: bfloat16 [7168, 4864], P(None, 'tensor'), may hold values from -0.0625 to 0.0625
- dense_down: bfloat16 [4864, 7168], P('tensor'), may hold values from -0.078125 to 0.078125
- expert_gate: bfloat16 [8, 7168, 4864], P('expert', None, 'tensor'), may hold values from -0.0625 to 0.0625
- expert_up: bfloat16 [8, 7168, 4864], P('expert', None, 'tensor'), may hold values from -0.0625 to 0.0625
- expert_down: bfloat16 [8, 4864, 7168], P('expert', 'tensor'), may hold values from -0.078125 to 0.078125
Outputs:
- mixed: bfloat16 [1024, 7168], P(('expert', 'tensor'))
The draws below stay inside these ranges and needn't reach their ends.
Inputs may be any that keep to these rules, and one draw needn't show every extreme that they name: route_ids names two different experts for every token; in each aligned block of 128 rows no expert is named more than 64 times, a bound that some block reaches.
All inputs are finite; a program needn't handle non-finite values.
Results may differ from the reference program's by a relative error of at most 0.015.
Values may be sent and summed in bfloat16 or wider, within the bound.
A program may use at most 128 MiB of HBM per device.

```python
import math
import jax
import jax.numpy as jnp
import numpy as np
from jax import lax

D = 7168
FF = 4864
FFE = 4864
TOK_GROUP = 128
TOKENS = 1024
EXPERTS = 8
CAP = 64
FF_DEV = 304
FFE_DEV = 304
N_EXPERT = 8
N_TENSOR = 16


def plant(result, stream_key, least, top_value):
    longest = result.shape.index(max(result.shape))
    spots = []
    for shift in (0, 1):
        where = [jax.random.randint(jax.random.fold_in(stream_key, axis), (), 0, length) for axis, length in enumerate(result.shape)]
        where[longest] = (where[longest] + shift) % result.shape[longest]
        spots.append(tuple(where))
    return result.at[spots[0]].set(least).at[spots[1]].set(top_value)


def levels(stream_key, shape, split, low, top_value):
    loudness, own = 1.0, jax.random.fold_in(stream_key, 6)
    for axis_at, blocks in split:
        draws = jnp.exp(jax.random.uniform(jax.random.fold_in(own, axis_at), (blocks,), jnp.float32, low / len(split), top_value / len(split)))
        loudness = loudness * jnp.repeat(draws, shape[axis_at] // blocks).reshape([-1 if axis == axis_at else 1 for axis in range(len(shape))])
    return loudness


def assign_block(stream_key, own, number, rows, count, top, reach, slope):
    sequence = jax.random.permutation(stream_key, count)
    packed, common = load_shares(count, rows * top, reach, slope, True), load_shares(count, rows * top, reach, slope, False)
    places = jnp.arange(count)

    def named(tallies, rotation):
        used = int((tallies > 0).sum())
        fixed = max(1, used // 4)
        moved = fixed + (places - fixed + rotation * (used - fixed)) % max(1, count - fixed)
        return jnp.zeros((count,), jnp.int32).at[sequence[jnp.where(places < fixed, places, moved)]].set(jnp.asarray(tallies, jnp.int32))

    tallies = jnp.where(number % 4 == 0, named(packed, number // 4), named(common, number - number // 4 - 1))
    mixed = jax.random.permutation(jax.random.fold_in(own, 3), count)
    source_of, taker = mixed[0:count // 2 * 2:2], mixed[1:count // 2 * 2:2]
    slack = jnp.minimum(tallies[source_of] - 1, reach - tallies[taker]) // 2
    slack = jnp.where((source_of == sequence[0]) | (taker == sequence[0]) | (tallies[taker] == 0), 0, jnp.maximum(slack, 0))
    moved = jax.random.randint(jax.random.fold_in(own, 4), (count // 2,), 0, 1 << 20) % (slack + 1)
    tallies = tallies.at[source_of].add(-moved).at[taker].add(moved)
    labels = jnp.searchsorted(jnp.cumsum(tallies), jnp.arange(rows * top), side="right").astype(jnp.int32)
    listing = labels.reshape(top, rows).T
    listing = listing[jax.random.permutation(jax.random.fold_in(own, 1), rows)]
    rotation = jax.random.randint(jax.random.fold_in(own, 2), (rows, 1), 0, top)
    return jnp.take_along_axis(listing, (jnp.arange(top)[None, :] + rotation) % top, axis=1)


def load_shares(amount, total, limit, skew, full):
    loads = [(1 << 20) // math.isqrt(grade ** skew) + 1 for grade in range(1, amount + 1)]
    largest = limit if full else min(limit, max(-(-total // amount), total * loads[0] // sum(loads)))
    least = 1 if total - largest >= amount - 1 else 0
    holding, spare = [largest] + [least] * (amount - 1), total - largest - least * (amount - 1)
    while spare > 0:
        candidates = [i for i in range(1, amount) if holding[i] < largest] or [i for i in range(1, amount) if holding[i] < limit]
        whole, left = sum([loads[i] for i in candidates]), spare
        for i in candidates:
            addition = min(limit - holding[i], max(1, left * loads[i] // whole), spare)
            holding[i] = holding[i] + addition
            spare = spare - addition
    return np.array(holding)


def gaussian(own_key, shape, deviation, reach, cuts=(), kind=jnp.bfloat16):
    entries = deviation * jax.random.normal(own_key, shape, jnp.float32)
    if cuts:
        entries = entries * levels(own_key, shape, cuts, -0.22, 0.18)
    return jnp.clip(entries, -reach, reach).astype(kind)


def setup_inputs(seed: int = 0) -> dict:
    keys = jax.random.split(jax.random.key(seed), 11)
    tokens = gaussian(keys[0], (TOKENS, D), 1.0, 6.0, ((0, 128),))
    route_ids_keys = jax.random.split(jax.random.fold_in(keys[1], 1), TOKENS // TOK_GROUP)
    route_ids_turns = jax.random.permutation(jax.random.fold_in(keys[1], 3), TOKENS // TOK_GROUP)
    route_ids = jax.vmap(lambda own, number: assign_block(jax.random.fold_in(keys[1], 2), own, number, TOK_GROUP, EXPERTS, 2, CAP, 2))(route_ids_keys, route_ids_turns).reshape((TOKENS, 2))
    route_gain = plant(jax.random.randint(keys[2], (TOKENS, 2), 1, 1024), jax.random.fold_in(keys[2], 1), 1, 1023).astype(jnp.int32)
    norm_gain = jnp.clip(1.0 + 0.18 * jax.random.normal(keys[3], (D,), jnp.float32), 0.1, 1.9)
    dense_gate = gaussian(keys[4], (D, FF), D ** -0.5, 0.0625, ((1, 16),))
    dense_up = gaussian(keys[5], (D, FF), D ** -0.5, 0.0625, ((1, 16),))
    dense_down = gaussian(keys[6], (FF, D), FF ** -0.5, 0.078125, ((0, 16),))
    expert_gate = gaussian(keys[7], (EXPERTS, D, FFE), D ** -0.5, 0.0625, ((0, 8), (2, 16)))
    expert_up = gaussian(keys[8], (EXPERTS, D, FFE), D ** -0.5, 0.0625, ((0, 8), (2, 16)))
    expert_down = gaussian(keys[9], (EXPERTS, FFE, D), FFE ** -0.5, 0.078125, ((0, 8), (1, 16)))
    return dict(tokens=tokens, route_ids=route_ids, route_gain=route_gain, norm_gain=norm_gain, dense_gate=dense_gate, dense_up=dense_up, dense_down=dense_down, expert_gate=expert_gate, expert_up=expert_up, expert_down=expert_down)


def reference(tokens, route_ids, route_gain, norm_gain, dense_gate, dense_up, dense_down, expert_gate, expert_up, expert_down):
    floats = tokens.astype(jnp.float32)
    normed = (floats * lax.rsqrt(lax.optimization_barrier(jnp.mean(floats * floats, axis=1, keepdims=True)) + 1e-05) * norm_gain).astype(jnp.bfloat16)
    gate_vals = jnp.dot(normed, dense_gate, preferred_element_type=jnp.float32)
    up_vals = jnp.dot(normed, dense_up, preferred_element_type=jnp.float32)
    dense_hidden = (jax.nn.silu(gate_vals) * up_vals).astype(jnp.bfloat16)
    hidden_groups = dense_hidden.reshape(TOKENS, N_TENSOR, FF_DEV).astype(jnp.float32)
    down_groups = dense_down.reshape(N_TENSOR, FF_DEV, D).astype(jnp.float32)
    dense_part = jnp.einsum('tgf,gfd->gtd', hidden_groups, down_groups)
    blocks = route_ids.reshape(N_EXPERT, TOK_GROUP * 2)
    onehot = (blocks[:, :, None] == jnp.arange(EXPERTS, dtype=jnp.int32)[None, None, :]).astype(jnp.int32)
    slot_rank = lax.optimization_barrier(jnp.sum(onehot * (jnp.cumsum(onehot, axis=1) - 1), axis=2))
    flat_slot = (jnp.arange(N_EXPERT, dtype=jnp.int32)[:, None] * CAP + slot_rank).reshape(-1).astype(jnp.int32)
    flat_ids = route_ids.reshape(-1).astype(jnp.int32)
    flat_row = (jnp.arange(TOKENS * 2, dtype=jnp.int32) // 2).astype(jnp.int32)
    flat_weight = route_gain.reshape(-1).astype(jnp.float32) / 1024.0
    row_table = jnp.zeros((EXPERTS, N_EXPERT * CAP), jnp.int32).at[flat_ids, flat_slot].set(flat_row)
    scale_table = jnp.zeros((EXPERTS, N_EXPERT * CAP), jnp.float32).at[flat_ids, flat_slot].set(flat_weight)

    def one_expert(combined, expert_index):
        rows_used = row_table[expert_index]
        inputs = normed[rows_used]
        gate_e = jnp.dot(inputs, expert_gate[expert_index], preferred_element_type=jnp.float32)
        up_e = jnp.dot(inputs, expert_up[expert_index], preferred_element_type=jnp.float32)
        hidden_e = (jax.nn.silu(gate_e) * up_e).astype(jnp.bfloat16)
        hidden_e = hidden_e.reshape(N_EXPERT * CAP, N_TENSOR, FFE_DEV).astype(jnp.float32)
        down_e = expert_down[expert_index].reshape(N_TENSOR, FFE_DEV, D).astype(jnp.float32)
        partial_e = jnp.einsum('rgf,gfd->grd', hidden_e, down_e).astype(jnp.bfloat16)
        weighted = scale_table[expert_index][None, :, None] * partial_e.astype(jnp.float32)
        return (combined.at[:, rows_used].add(weighted), None)
    combined, _ = lax.scan(one_expert, dense_part, jnp.arange(EXPERTS, dtype=jnp.int32))
    return (floats + lax.optimization_barrier(jnp.sum(combined, axis=0))).astype(jnp.bfloat16)
```

```python
import jax
import jax.numpy as jnp
from jax import lax
from jax.experimental import pallas as pl
from jax.experimental.pallas import tpu as pltpu
from jax.sharding import PartitionSpec as P

F32, BF16 = jnp.float32, jnp.bfloat16
WIDTHS = (1280, 1152, 1152)
STARTS = (0, 1280, 2432)
HALF = 3584
GATHER = ((1, 2, 0), (2, 0, 1), (0, 1, 2))
REDUCE = ((0, 1, 2), (1, 2, 0), (2, 0, 1))
STEPS = (1, 3, 2)
ALL = slice(None)


def position():
    e, t = lax.axis_index("expert"), lax.axis_index("tensor")
    x = lax.div(t, 8) * 2 + lax.div(e, 4)
    y = lax.rem(lax.div(t, 2), 4)
    z = lax.rem(e, 4)
    return (x, y, z), lax.rem(t, 2)


def device(pos, core):
    x, y, z = pos
    return (lax.rem(x, 2) * 4 + z, (lax.div(x, 2) * 4 + y) * 2 + core)


def moved(pos, axis, step):
    return tuple(lax.rem(p + step, 4) if a == axis else p for a, p in enumerate(pos))


def at(parts):
    return tuple(parts[a] for a in range(3))


def greet(pos, core):
    barrier = pltpu.get_barrier_semaphore()
    others = [device(moved(pos, a, s), core) for a in range(3) for s in STEPS]
    others.append(device(pos, 1 - core))
    for other in others:
        pl.semaphore_signal(barrier, inc=1, device_id=other, device_id_type=pl.DeviceIdType.MESH)
    pl.semaphore_wait(barrier, len(others))


def remote(src, dst, send, recv, target):
    return pltpu.make_async_remote_copy(
        src_ref=src,
        dst_ref=dst,
        send_sem=send,
        recv_sem=recv,
        device_id=target,
        device_id_type=pl.DeviceIdType.MESH,
    )


def dot(a, b):
    return jnp.dot(a, b, preferred_element_type=F32)


def hidden_kernel(
    tok, ids, gains, gain, wg_e, wu_e, wg_d, wu_d,
    he, hd, weight,
    x0, x1, x2, vg_e, vu_e, vg_d, vu_d, acc_g, acc_u, mine, other,
    w_sem, pair_s, pair_r, s1, r1, s2, r2, s3, r3, fs, fr,
):
    xs = (x0, x1, x2)
    pos, core = position()
    rest = 1 - core
    sibling = device(pos, rest)
    loads = [
        pltpu.make_async_copy(src, dst, w_sem.at[i])
        for i, (src, dst) in enumerate(((wg_e, vg_e), (wu_e, vu_e), (wg_d, vg_d), (wu_d, vu_d)))
    ]
    for load in loads:
        load.start()
    floats = tok[...].astype(F32)
    normed = floats * lax.rsqrt(jnp.mean(floats * floats, axis=1, keepdims=True) + 1e-05) * gain[...]
    lane = lax.broadcasted_iota(jnp.int32, (8, 128), 1)
    extra = jnp.zeros((8, 128), F32)
    for k in range(2):
        g = gains[:, k : k + 1]
        who = ids[:, k : k + 1]
        high = lax.shift_right_logical(g, 5)
        low = g - high * 32
        extra = extra + jnp.where(lane == who, high.astype(F32), 0.0)
        extra = extra + jnp.where(lane == who + 8, low.astype(F32), 0.0)
    for h in range(2):
        mine[h, :, :HALF] = normed[:, h * HALF : (h + 1) * HALF].astype(BF16)
        mine[h, :, HALF:] = extra.astype(BF16)
    greet(pos, core)
    sends = []

    def go(copy):
        copy.start()
        sends.append(copy)

    swap = remote(mine.at[rest], other, pair_s, pair_r, sibling)
    go(swap)
    swap.wait_recv()
    a, b = mine[core].astype(F32), other[...].astype(F32)
    first = core == 0
    slab = jnp.concatenate([jnp.where(first, a, b), jnp.where(first, b, a)], axis=0).astype(BF16)
    for j in range(3):
        wide = xs[j].shape[-1]
        xs[j][(core, *pos)] = slab[:, STARTS[j] : STARTS[j] + wide]

    def copy(j, idx, sem_s, sem_r, target, half=None):
        ref = xs[j].at[(core if half is None else half, *idx)]
        return remote(ref, ref, sem_s, sem_r, target)

    for j in range(3):
        axis = GATHER[j][0]
        for k, d in enumerate(STEPS):
            go(copy(j, pos, s1.at[j, k], r1.at[j, k], device(moved(pos, axis, d), core)))
    acc_g[...] = jnp.zeros_like(acc_g)
    acc_u[...] = jnp.zeros_like(acc_u)

    def block(j, phase, step, part=ALL):
        a1, a2, a3 = GATHER[j]
        parts = {a1: part, a2: pos[a2], a3: pos[a3]}
        if phase == 2:
            parts[a2] = lax.rem(pos[a2] + step, 4)
        if phase == 3:
            parts[a2] = ALL
            parts[a3] = lax.rem(pos[a3] + step, 4)
        return at(parts)

    def forward(j, n, idx):
        go(copy(j, idx, fs.at[j, n], fr.at[j, n], sibling))

    def forwarded(j, n, idx):
        copy(j, idx, fs.at[j, n], fr.at[j, n], sibling, rest).wait_recv()

    lower, upper = slice(0, 2), slice(2, 4)

    def spread(j, phase, ss, rr):
        axis = GATHER[j][phase - 1]
        for k, d in enumerate((1, 3)):
            go(copy(j, block(j, phase, 0), ss.at[j, k], rr.at[j, k], device(moved(pos, axis, d), core)))

    def relay(j, phase, ss, rr, n):
        axis = GATHER[j][phase - 1]
        for k, (came, part, d) in enumerate(((3, lower, 1), (1, upper, 3))):
            copy(j, block(j, phase, came), ss.at[j, k], rr.at[j, k], sibling).wait_recv()
            go(copy(j, block(j, phase, came, part), ss.at[j, 2 + k], rr.at[j, 2 + k], device(moved(pos, axis, d), core)))
            forward(j, n + k, block(j, phase, came))

    def finish(j, phase, ss, rr, n):
        for k, part in enumerate((lower, upper)):
            copy(j, block(j, phase, 2, part), ss.at[j, 2 + k], rr.at[j, 2 + k], sibling).wait_recv()
        forward(j, n, block(j, phase, 2))

    def add(j, idx, half):
        rows = xs[j][(half, *idx)].reshape(256, xs[j].shape[-1])[:, : WIDTHS[j]]
        span = pl.ds(pl.multiple_of(half * HALF + STARTS[j], 128), WIDTHS[j])
        for acc, w in ((acc_g, vg_e), (acc_u, vu_e)):
            acc[idx] += dot(rows, w[span, :]).reshape(4, 4, 16, 304)

    for j in range(3):
        axis = GATHER[j][0]
        for k, d in enumerate(STEPS):
            copy(j, moved(pos, axis, 4 - d), s1.at[j, k], r1.at[j, k], sibling).wait_recv()
        spread(j, 2, s2, r2)
        forward(j, 0, block(j, 1, 0))
    for j in range(3):
        relay(j, 2, s2, r2, 1)
    for j in range(3):
        finish(j, 2, s2, r2, 3)
        spread(j, 3, s3, r3)
    for load in loads:
        load.wait()
    for j in range(3):
        add(j, block(j, 3, 0), core)
    for j in range(3):
        forwarded(j, 0, block(j, 1, 0))
        for n, step in ((1, 3), (2, 1), (3, 2)):
            forwarded(j, n, block(j, 2, step))
        add(j, block(j, 3, 0), rest)
    for j in range(3):
        relay(j, 3, s3, r3, 4)
    for j in range(3):
        add(j, block(j, 3, 3), core)
        add(j, block(j, 3, 1), core)
    for j in range(3):
        forwarded(j, 4, block(j, 3, 3))
        add(j, block(j, 3, 3), rest)
        forwarded(j, 5, block(j, 3, 1))
        add(j, block(j, 3, 1), rest)
    for j in range(3):
        finish(j, 3, s3, r3, 6)
        add(j, block(j, 3, 2), core)
    for j in range(3):
        forwarded(j, 6, block(j, 3, 2))
        add(j, block(j, 3, 2), rest)

    x_low = lax.rem(pos[0], 2)
    for xh in range(2):
        g = jnp.zeros((64, 304), F32)
        u = jnp.zeros((64, 304), F32)
        for j in range(3):
            for h in range(2):
                rows = xs[j][h, x_low + 2 * xh, :, pos[2]].reshape(64, xs[j].shape[-1])[:, : WIDTHS[j]]
                span = pl.ds(h * HALF + STARTS[j], WIDTHS[j])
                g = g + dot(rows, vg_d[span, :])
                u = u + dot(rows, vu_d[span, :])
        hd[xh] = (g / (1.0 + jnp.exp(-g)) * u).astype(BF16).reshape(4, 16, 304)
    e = lax.axis_index("expert")
    lanes = lax.broadcasted_iota(jnp.int32, (256, 128), 1)
    pick = jnp.where(lanes == e, 32.0, 0.0) + jnp.where(lanes == e + 8, 1.0, 0.0)

    def tail(x, carry):
        g = acc_g[x].reshape(256, 304)
        u = acc_u[x].reshape(256, 304)
        he[x] = (g / (1.0 + jnp.exp(-g)) * u).astype(BF16).reshape(4, 4, 16, 304)
        pieces = x2[core, x, :, :, :, WIDTHS[2] :].reshape(256, 128).astype(F32)
        weight[x] = (jnp.sum(pieces * pick, axis=1, keepdims=True) * (1.0 / 1024.0)).reshape(4, 4, 16, 1)
        return carry

    lax.fori_loop(0, 4, tail, 0)
    for c in sends:
        c.wait_send()


def sum_kernel(
    he, hd, weight, tok, wd_e, wd_d,
    out,
    vd_e, vd_d, z0, z1, z2, o0, o1, o2, i0, i1, i2,
    a0, a1, a2, b0, b1, b2, c0, c1, c2, d0, d1, d2, t0, t1, t2, fin_s, fin_r,
    w_sem, ps, pr, s1, r1, s2, r2, s3, r3, f_s, f_r,
):
    zs, outs, ins = (z0, z1, z2), (o0, o1, o2), (i0, i1, i2)
    half1, full1, half2, full2, last = (a0, a1, a2), (b0, b1, b2), (c0, c1, c2), (d0, d1, d2), (t0, t1, t2)
    pos, core = position()
    rest = 1 - core
    sibling = device(pos, rest)
    loads = [pltpu.make_async_copy(wd_e, vd_e, w_sem.at[0]), pltpu.make_async_copy(wd_d, vd_d, w_sem.at[1])]
    for load in loads:
        load.start()
    greet(pos, core)
    for load in loads:
        load.wait()
    sends = []

    def go(copy):
        copy.start()
        sends.append(copy)

    def where(j, step, part=ALL):
        b1, b2, b3 = REDUCE[j]
        return at({b1: lax.rem(pos[b1] + step, 4), b2: part, b3: ALL})

    def inner(j, step, part=ALL):
        b1, b2, b3 = REDUCE[j]
        return at({b1: pos[b1], b2: lax.rem(pos[b2] + step, 4), b3: part})

    x_low = lax.rem(pos[0], 2)

    def produce(ref, j, step, half):
        cols = pl.ds(pl.multiple_of(half * HALF + STARTS[j], 128), WIDTHS[j])
        idx = where(j, step)
        part = dot(he[idx].reshape(256, 304), vd_e[:, cols]).astype(BF16).astype(F32)
        part = part * weight[idx].reshape(256, 1)
        ref[idx] = part.astype(BF16).reshape(4, 4, 16, WIDTHS[j])
        axis = REDUCE[j][0]
        if axis == 0:
            if step % 2:
                return
            x = idx[0]
            places = [((x, ALL, pos[2]), (lax.div(x, 2), ALL), 64, (4, 16))]
        elif axis == 1:
            places = [((x_low + 2 * k, idx[1], pos[2]), (k, idx[1]), 16, (16,)) for k in range(2)]
        else:
            if step:
                return
            places = [((x_low + 2 * k, ALL, pos[2]), (k, ALL), 64, (4, 16)) for k in range(2)]
        for spot, src, rows, shape in places:
            dense = dot(hd[src].reshape(rows, 304), vd_d[:, cols])
            ref[spot] = (ref[spot].astype(F32) + dense.reshape(*shape, WIDTHS[j])).astype(BF16)

    def gain(j, idx, *others):
        total = zs[j][idx].astype(F32)
        for other in others:
            total = total + other[...].astype(F32)
        zs[j][idx] = total.astype(BF16)

    def halves(j, phase, place, bufs, ss, rr):
        axis = REDUCE[j][phase]
        for k, (part, d) in enumerate(((slice(0, 2), 1), (slice(2, 4), 3))):
            go(remote(zs[j].at[place(j, 2, part)], bufs[j].at[k], ss.at[j, k], rr.at[j, k], device(moved(pos, axis, d), core)))

    def wholes(j, phase, place, step, bufs, fulls, ss, rr):
        axis = REDUCE[j][phase]
        k, part = (0, slice(0, 2)) if step == 1 else (1, slice(2, 4))
        remote(bufs[j].at[k], bufs[j].at[k], ss.at[j, k], rr.at[j, k], sibling).wait_recv()
        gain(j, place(j, step, part), bufs[j].at[k])
        go(remote(zs[j].at[place(j, step)], fulls[j].at[k], ss.at[j, 2 + k], rr.at[j, 2 + k], device(moved(pos, axis, step), core)))

    def close(j, place, fulls, ss, rr):
        for k in range(2):
            remote(fulls[j].at[k], fulls[j].at[k], ss.at[j, 2 + k], rr.at[j, 2 + k], sibling).wait_recv()
        gain(j, place(j, 0), fulls[j].at[0], fulls[j].at[1])

    for n, step in enumerate((2, 1, 3, 0)):
        for j in range(3):
            produce(outs[j], j, step, rest)
            idx = where(j, step)
            go(remote(outs[j].at[idx], ins[j].at[idx], ps.at[j, n], pr.at[j, n], sibling))
        for j in range(3):
            produce(zs[j], j, step, core)
        for j in range(3):
            idx = where(j, step)
            remote(outs[j].at[idx], ins[j].at[idx], ps.at[j, n], pr.at[j, n], sibling).wait_recv()
            gain(j, idx, ins[j].at[idx])
            if step == 2:
                halves(j, 0, where, half1, s1, r1)
            elif step:
                wholes(j, 0, where, step, half1, full1, s1, r1)
    for j in range(3):
        close(j, where, full1, s1, r1)
        halves(j, 1, inner, half2, s2, r2)
    for j in range(3):
        for step in (1, 3):
            wholes(j, 1, inner, step, half2, full2, s2, r2)
    for j in range(3):
        close(j, inner, full2, s2, r2)
        axis = REDUCE[j][2]
        for k, d in enumerate(STEPS):
            there = moved(pos, axis, d)
            go(remote(zs[j].at[there], last[j].at[k], s3.at[j, k], r3.at[j, k], device(there, core)))
    first = core == 0
    keep = []
    for j in range(3):
        total = zs[j][pos].astype(F32)
        for k in range(3):
            remote(last[j].at[k], last[j].at[k], s3.at[j, k], r3.at[j, k], sibling).wait_recv()
            total = total + last[j][k].astype(F32)
        top, bottom = total[:8], total[8:]
        keep.append(jnp.where(first, top, bottom))
        fin_s[:, STARTS[j] : STARTS[j] + WIDTHS[j]] = jnp.where(first, bottom, top)
    swap = remote(fin_s, fin_r, f_s, f_r, sibling)
    go(swap)
    for j in range(3):
        cols = pl.ds(pl.multiple_of(core * HALF + STARTS[j], 128), WIDTHS[j])
        out[:, cols] = (tok[:, cols].astype(F32) + keep[j]).astype(BF16)
    swap.wait_recv()
    cols = pl.ds(pl.multiple_of(rest * HALF, 128), HALF)
    out[:, cols] = (tok[:, cols].astype(F32) + fin_r[...]).astype(BF16)
    for c in sends:
        c.wait_send()


def per_device(
    tokens, route_ids, route_gain, norm_gain, dense_gate, dense_up, dense_down, expert_gate, expert_up, expert_down
):
    vmem = pl.BlockSpec(memory_space=pltpu.VMEM)
    hbm = pl.BlockSpec(memory_space=pl.ANY)
    dma = pltpu.SemaphoreType.DMA
    d, f = dense_gate.shape
    gathered = [pltpu.VMEM((2, 4, 4, 4, 16, w + (128 if j == 2 else 0)), BF16) for j, w in enumerate(WIDTHS)]
    he, hd, weight = pl.pallas_call(
        hidden_kernel,
        out_shape=(
            jax.ShapeDtypeStruct((4, 4, 4, 16, f), BF16),
            jax.ShapeDtypeStruct((2, 4, 16, f), BF16),
            jax.ShapeDtypeStruct((4, 4, 4, 16, 1), F32),
        ),
        in_specs=[vmem] * 4 + [hbm] * 4,
        out_specs=(vmem,) * 3,
        scratch_shapes=gathered
        + [pltpu.VMEM((d, f), BF16)] * 4
        + [pltpu.VMEM((4, 4, 4, 16, f), F32)] * 2
        + [pltpu.VMEM((2, 8, HALF + 128), BF16), pltpu.VMEM((8, HALF + 128), BF16)]
        + [dma((4,)), dma, dma]
        + [dma((3, 3))] * 2
        + [dma((3, 4))] * 4
        + [dma((3, 7))] * 2,
        compiler_params=pltpu.CompilerParams(
            collective_id=0, has_side_effects=True, vmem_limit_bytes=60 * 1024 * 1024
        ),
        name="gather_hidden",
    )(
        tokens, route_ids, route_gain, norm_gain.reshape(1, d),
        expert_gate.reshape(d, f), expert_up.reshape(d, f), dense_gate, dense_up,
    )

    def sized(*lead):
        return [pltpu.VMEM((*lead, w), BF16) for w in WIDTHS]

    return pl.pallas_call(
        sum_kernel,
        out_shape=jax.ShapeDtypeStruct(tokens.shape, BF16),
        in_specs=[vmem] * 4 + [hbm] * 2,
        out_specs=vmem,
        scratch_shapes=[pltpu.VMEM((f, d), BF16)] * 2
        + sized(4, 4, 4, 16)
        + sized(4, 4, 4, 16)
        + sized(4, 4, 4, 16)
        + [pltpu.VMEM(halved(j, w), BF16) for j, w in enumerate(WIDTHS)]
        + sized(2, 4, 4, 16)
        + sized(2, 2, 16)
        + sized(2, 4, 16)
        + sized(3, 16)
        + [pltpu.VMEM((8, HALF), F32)] * 2
        + [dma((2,))]
        + [dma((3, 4))] * 6
        + [dma((3, 3))] * 2
        + [dma, dma],
        compiler_params=pltpu.CompilerParams(
            collective_id=1, has_side_effects=True, vmem_limit_bytes=60 * 1024 * 1024
        ),
        name="down_sum",
    )(he, hd, weight, tokens, expert_down.reshape(f, d), dense_down)


def halved(j, width):
    b1, b2, _ = REDUCE[j]
    return (2, *(2 if a == b2 else 4 for a in range(3) if a != b1), 16, width)


def solution(mesh):
    rows = P(("expert", "tensor"), None)
    return jax.shard_map(
        per_device,
        mesh=mesh,
        in_specs=(
            rows, rows, rows, P(),
            P(None, "tensor"), P(None, "tensor"), P("tensor", None),
            P("expert", None, "tensor"), P("expert", None, "tensor"), P("expert", "tensor", None),
        ),
        out_specs=rows,
        check_vma=False,
    )
```

```python
import jax
import jax.numpy as jnp
from jax import lax
from jax.experimental import pallas as pl
from jax.experimental.pallas import tpu as pltpu
from jax.sharding import PartitionSpec as P

F32, BF16 = jnp.float32, jnp.bfloat16
WIDTHS = (1280, 1152, 1152)
STARTS = (0, 1280, 2432)
HALF = 3584
GATHER = ((1, 2, 0), (2, 0, 1), (0, 1, 2))
REDUCE = ((0, 1, 2), (1, 2, 0), (2, 0, 1))
STEPS = (1, 3, 2)
LINES = (0, 3, 1, 2)
PLANES = (0, 3, 1, 2)
ALL = slice(None)


def position():
    e, t = lax.axis_index("expert"), lax.axis_index("tensor")
    x = lax.div(t, 8) * 2 + lax.div(e, 4)
    y = lax.rem(lax.div(t, 2), 4)
    z = lax.rem(e, 4)
    return (x, y, z), lax.rem(t, 2)


def device(pos, core):
    x, y, z = pos
    return (lax.rem(x, 2) * 4 + z, (lax.div(x, 2) * 4 + y) * 2 + core)


def moved(pos, axis, step):
    return tuple(lax.rem(p + step, 4) if a == axis else p for a, p in enumerate(pos))


def at(parts):
    return tuple(parts[a] for a in range(3))


def greet(pos, core):
    barrier = pltpu.get_barrier_semaphore()
    others = [device(moved(pos, a, s), core) for a in range(3) for s in STEPS]
    others.append(device(pos, 1 - core))
    for other in others:
        pl.semaphore_signal(barrier, inc=1, device_id=other, device_id_type=pl.DeviceIdType.MESH)
    pl.semaphore_wait(barrier, len(others))


def remote(src, dst, send, recv, target):
    return pltpu.make_async_remote_copy(
        src_ref=src,
        dst_ref=dst,
        send_sem=send,
        recv_sem=recv,
        device_id=target,
        device_id_type=pl.DeviceIdType.MESH,
    )


def dot(a, b):
    return jnp.dot(a, b, preferred_element_type=F32)


def dot_t(a, b):
    return lax.dot_general(a, b, (((1,), (1,)), ((), ())), preferred_element_type=F32)


def block_kernel(
    tok, ids, gains, gain, wg_e, wu_e, wg_d, wu_d, wd_e, wd_d,
    out,
    x0, x1, x2, mine, other,
    down_e, down_d, he, he_in, heb, hd, hd_in, hdb, weight,
    a0, a1, a2, b0, b1, b2, c0, c1, c2, d0, d1, d2, t0, t1, t2, fin_s, fin_r,
    w_sem, down_s, down_r, pair_s, pair_r, g1s, g1r, g2s, g2r, g3s, g3r, fs, fr,
    he_s, he_r, hd_s, hd_r, s1, r1, s2, r2, s3, r3, f_s, f_r,
):
    xs = (x0, x1, x2)
    pos, core = position()
    rest = 1 - core
    sibling = device(pos, rest)
    own_cols = pl.ds(pl.multiple_of(core * HALF, 128), HALF)
    rest_cols = pl.ds(pl.multiple_of(rest * HALF, 128), HALF)
    x_low = lax.rem(pos[0], 2)
    first = core == 0
    lower, upper = slice(0, 2), slice(2, 4)
    sends = []

    def go(copy):
        copy.start()
        sends.append(copy)

    def settle():
        for copy in sends:
            copy.wait_send()
        sends.clear()

    def gather(up_e, up_d, acc, acc_d):
        top, low = pl.ds(0, 304), pl.ds(304, 304)
        loads = [
            pltpu.make_async_copy(src, dst, w_sem.at[i])
            for i, (src, dst) in enumerate((
                (wg_e, up_e.at[top]), (wu_e, up_e.at[low]), (wg_d, up_d.at[top]), (wu_d, up_d.at[low]),
                (wd_e.at[:, own_cols], down_e.at[top]), (wd_d.at[:, own_cols], down_d.at[top]),
            ))
        ]
        for load in loads:
            load.start()
        floats = tok[...].astype(F32)
        normed = floats * lax.rsqrt(jnp.mean(floats * floats, axis=1, keepdims=True) + 1e-05) * gain[...]
        lane = lax.broadcasted_iota(jnp.int32, (8, 128), 1).astype(F32)
        same = lax.broadcasted_iota(jnp.int32, (8, 8), 0) == lax.broadcasted_iota(jnp.int32, (8, 8), 1)
        extra = jnp.zeros((8, 128), F32)
        for k in range(2):
            g, who = (
                jnp.sum(jnp.where(same, ref[k : k + 1, :].astype(F32), 0.0), axis=1, keepdims=True)
                for ref in (gains, ids)
            )
            high = jnp.floor(g * (1.0 / 32.0))
            extra = extra + jnp.where(lane == who, high, 0.0)
            extra = extra + jnp.where(lane == who + 8.0, g - high * 32.0, 0.0)
        for h in range(2):
            mine[h, :, :HALF] = normed[:, h * HALF : (h + 1) * HALF].astype(BF16)
            mine[h, :, HALF:] = extra.astype(BF16)
        greet(pos, core)
        swap = remote(mine.at[rest], other, pair_s, pair_r, sibling)
        go(swap)
        lends = [
            remote(src.at[:, rest_cols], dst.at[low], down_s.at[i], down_r.at[i], sibling)
            for i, (src, dst) in enumerate(((wd_e, down_e), (wd_d, down_d)))
        ]
        swap.wait_recv()
        a, b = mine[core].astype(F32), other[...].astype(F32)
        slab = jnp.concatenate([jnp.where(first, a, b), jnp.where(first, b, a)], axis=0).astype(BF16)
        for j in range(3):
            wide = xs[j].shape[-1]
            xs[j][(core, *pos)] = slab[:, STARTS[j] : STARTS[j] + wide]

        def copy(j, idx, sem_s, sem_r, target, half=None):
            ref = xs[j].at[(core if half is None else half, *idx)]
            return remote(ref, ref, sem_s, sem_r, target)

        for j in range(3):
            axis = GATHER[j][0]
            for k, d in enumerate(STEPS):
                go(copy(j, pos, g1s.at[j, k], g1r.at[j, k], device(moved(pos, axis, d), core)))
        for lend in lends:
            go(lend)
        acc[...] = jnp.zeros_like(acc)
        acc_d[...] = jnp.zeros_like(acc_d)

        sides = ((3, lower, 1), (1, upper, 3))

        def line(j, n, m, part=ALL):
            a1, a2, a3 = GATHER[j]
            return at({a1: part, a2: lax.rem(pos[a2] + LINES[n], 4), a3: lax.rem(pos[a3] + PLANES[m], 4)})

        def plane(j, m):
            a1, a2, a3 = GATHER[j]
            return at({a1: ALL, a2: ALL, a3: lax.rem(pos[a3] + PLANES[m], 4)})

        def forward(j, n, m):
            go(copy(j, line(j, n, m), fs.at[j, n, m], fr.at[j, n, m], sibling))

        def forwarded(m):
            for j in range(3):
                for n in range(4):
                    copy(j, line(j, n, m), fs.at[j, n, m], fr.at[j, n, m], sibling, rest).wait_recv()

        def own(j, n):
            axis = GATHER[j][2]
            for k, d in enumerate((1, 3)):
                go(copy(j, line(j, n, 0), g3s.at[j, n, k], g3r.at[j, n, k], device(moved(pos, axis, d), core)))
            forward(j, n, 0)

        def relay(j, n):
            axis = GATHER[j][2]
            for k, (came, part, d) in enumerate(sides):
                m = 1 + k
                copy(j, line(j, n, m), g3s.at[j, n, k], g3r.at[j, n, k], sibling).wait_recv()
                target = device(moved(pos, axis, d), core)
                go(copy(j, line(j, n, m, part), g3s.at[j, n, 2 + k], g3r.at[j, n, 2 + k], target))
                forward(j, n, m)

        def add(j, idx, half):
            rows = xs[j][(half, *idx)].reshape(256, xs[j].shape[-1])[:, : WIDTHS[j]]
            span = pl.ds(pl.multiple_of(half * HALF + STARTS[j], 128), WIDTHS[j])
            acc[idx] += dot_t(rows, up_e[:, span]).reshape(4, 4, 16, 608)

        def add_dense(j):
            for h in range(2):
                rows = jnp.concatenate(
                    [
                        xs[j][h, x_low + 2 * k, :, pos[2]].reshape(64, xs[j].shape[-1])[:, : WIDTHS[j]]
                        for k in range(2)
                    ],
                    axis=0,
                )
                acc_d[...] += dot_t(rows, up_d[:, h * HALF + STARTS[j] : h * HALF + STARTS[j] + WIDTHS[j]])

        def adds(m, half):
            for j in range(3):
                add(j, plane(j, m), half)

        for j in range(3):
            axis = GATHER[j][0]
            for k, d in enumerate(STEPS):
                copy(j, moved(pos, axis, 4 - d), g1s.at[j, k], g1r.at[j, k], sibling).wait_recv()
            axis = GATHER[j][1]
            for k, d in enumerate((1, 3)):
                go(copy(j, line(j, 0, 0), g2s.at[j, k], g2r.at[j, k], device(moved(pos, axis, d), core)))
            own(j, 0)
        for j in range(3):
            axis = GATHER[j][1]
            for k, (came, part, d) in enumerate(sides):
                n = 1 + k
                copy(j, line(j, n, 0), g2s.at[j, k], g2r.at[j, k], sibling).wait_recv()
                target = device(moved(pos, axis, d), core)
                go(copy(j, line(j, n, 0, part), g2s.at[j, 2 + k], g2r.at[j, 2 + k], target))
                own(j, n)
        for j in range(3):
            relay(j, 0)
        for j in range(3):
            for k, part in enumerate((lower, upper)):
                copy(j, line(j, 3, 0, part), g2s.at[j, 2 + k], g2r.at[j, 2 + k], sibling).wait_recv()
            own(j, 3)
        for load in loads:
            load.wait()
        for j in range(3):
            relay(j, 1)
            add(j, plane(j, 0), core)
        for j in range(3):
            relay(j, 2)
        forwarded(0)
        adds(0, rest)
        add_dense(2)
        for j in range(3):
            relay(j, 3)
        adds(1, core)
        adds(2, core)

        def last(n):
            for j in range(3):
                for k, part in enumerate((lower, upper)):
                    copy(j, line(j, n, 3, part), g3s.at[j, n, 2 + k], g3r.at[j, n, 2 + k], sibling).wait_recv()
                forward(j, n, 3)

        last(0)
        last(1)
        forwarded(1)
        adds(1, rest)
        last(2)
        forwarded(2)
        adds(2, rest)
        last(3)
        adds(3, core)
        forwarded(3)
        adds(3, rest)

        def glu(v):
            g, u = v[:, :304], v[:, 304:]
            return (g / (1.0 + jnp.exp(-g)) * u).astype(BF16)

        e = lax.axis_index("expert")
        lanes = lax.broadcasted_iota(jnp.int32, (256, 128), 1)
        pick = jnp.where(lanes == e, 32.0, 0.0) + jnp.where(lanes == e + 8, 1.0, 0.0)
        trades = [remote(he.at[x], he_in.at[x], he_s.at[x], he_r.at[x], sibling) for x in range(4)]
        for x in range(4):
            he[x] = glu(acc[x].reshape(256, 608)).reshape(4, 4, 16, 304)
            go(trades[x])
        for x in range(4):
            pieces = x2[core, x, :, :, :, WIDTHS[2] :].reshape(256, 128).astype(F32)
            weight[x] = (jnp.sum(pieces * pick, axis=1, keepdims=True) * (1.0 / 1024.0)).reshape(4, 4, 16, 1)
        add_dense(0)
        add_dense(1)
        hd[...] = glu(acc_d[...])
        go(remote(hd, hd_in, hd_s, hd_r, sibling))
        for x in range(4):
            trades[x].wait_recv()
            heb[x] = jnp.concatenate([he[x].reshape(256, 304), he_in[x].reshape(256, 304)], axis=1).reshape(4, 4, 16, 608)
        for lend in lends:
            lend.wait_recv()
        settle()

    def reduce(z0, z1, z2, q0, q1, q2):
        zs, dense = (z0, z1, z2), (q0, q1, q2)
        half1, full1, half2, full2, last_in = (a0, a1, a2), (b0, b1, b2), (c0, c1, c2), (d0, d1, d2), (t0, t1, t2)

        def where(j, step):
            b1, b2, b3 = REDUCE[j]
            return at({b1: lax.rem(pos[b1] + step, 4), b2: ALL, b3: ALL})

        def produce(j, step):
            cols = slice(STARTS[j], STARTS[j] + WIDTHS[j])
            idx = where(j, step)
            part = dot(heb[idx].reshape(256, 608), down_e[:, cols]) * weight[idx].reshape(256, 1)
            zs[j][idx] = part.astype(BF16).reshape(4, 4, 16, WIDTHS[j])

        def produce_dense(j, step):
            idx = where(j, step)
            axis = REDUCE[j][0]
            places = []
            if axis == 0 and step % 2 == 0:
                places = [((idx[0], ALL, pos[2]), (lax.div(idx[0], 2), ALL))]
            elif axis == 1:
                places = [((x_low + 2 * k, idx[1], pos[2]), (k, idx[1])) for k in range(2)]
            elif axis == 2 and step == 0:
                places = [((x_low + 2 * k, ALL, pos[2]), (k, ALL)) for k in range(2)]
            for spot, src in places:
                zs[j][spot] = (zs[j][spot].astype(F32) + dense[j][src]).astype(BF16)

        def gain(j, idx, *others):
            total = zs[j][idx].astype(F32)
            for other in others:
                total = total + other[...].astype(F32)
            zs[j][idx] = total.astype(BF16)

        def row(j, step, r, part=ALL):
            b1, b2, b3 = REDUCE[j]
            return at({b1: lax.rem(pos[b1] + step, 4), b2: lax.rem(pos[b2] + r, 4), b3: part})

        def halves(j, step, r, axis, bufs, ss, rr):
            for k, (part, d) in enumerate(((lower, 1), (upper, 3))):
                go(remote(zs[j].at[row(j, step, r, part)], bufs.at[k], ss.at[k], rr.at[k], device(moved(pos, axis, d), core)))

        def whole(j, step, r, axis, k, bufs, fulls, ss, rr):
            part, d = ((lower, 1), (upper, 3))[k]
            remote(bufs.at[k], bufs.at[k], ss.at[k], rr.at[k], sibling).wait_recv()
            gain(j, row(j, step, r, part), bufs.at[k])
            go(remote(zs[j].at[row(j, step, r)], fulls.at[k], ss.at[2 + k], rr.at[2 + k], device(moved(pos, axis, d), core)))

        def close(j, r, fulls, ss, rr):
            for k in range(2):
                remote(fulls.at[k], fulls.at[k], ss.at[2 + k], rr.at[2 + k], sibling).wait_recv()
            gain(j, row(j, 0, r), fulls.at[0], fulls.at[1])

        def outer(j, n):
            return (half1[j].at[n], full1[j].at[n], s1.at[j, n], r1.at[j, n])

        def inner(j):
            return (half2[j], full2[j], s2.at[j], r2.at[j])

        order = (2, 1, 3, 0)
        for n, step in enumerate(order):
            for j in range(3):
                produce(j, step)
            if n == 0:
                remote(hd, hd_in, hd_s, hd_r, sibling).wait_recv()
                hdb[...] = jnp.concatenate([hd[...], hd_in[...]], axis=1)
                for j in range(3):
                    part = dot(hdb[...], down_d[:, STARTS[j] : STARTS[j] + WIDTHS[j]])
                    dense[j][...] = part.reshape(2, 4, 16, WIDTHS[j])
            for j in range(3):
                produce_dense(j, step)
                for i, r in enumerate(order):
                    bufs, fulls, ss, rr = outer(j, i)
                    if step == 2:
                        halves(j, 2, r, REDUCE[j][0], bufs, ss, rr)
                    elif step:
                        whole(j, step, r, REDUCE[j][0], n - 1, bufs, fulls, ss, rr)
        for i, r in enumerate(order):
            for j in range(3):
                _, fulls, ss, rr = outer(j, i)
                close(j, r, fulls, ss, rr)
                bufs, fulls, ss, rr = inner(j)
                if r == 2:
                    halves(j, 0, r, REDUCE[j][1], bufs, ss, rr)
                elif r:
                    whole(j, 0, r, REDUCE[j][1], i - 1, bufs, fulls, ss, rr)
        for j in range(3):
            _, fulls, ss, rr = inner(j)
            close(j, 0, fulls, ss, rr)
            axis = REDUCE[j][2]
            for k, d in enumerate(STEPS):
                there = moved(pos, axis, d)
                go(remote(zs[j].at[there], last_in[j].at[k], s3.at[j, k], r3.at[j, k], device(there, core)))
        keep = []
        for j in range(3):
            total = zs[j][pos].astype(F32)
            for k in range(3):
                remote(last_in[j].at[k], last_in[j].at[k], s3.at[j, k], r3.at[j, k], sibling).wait_recv()
                total = total + last_in[j][k].astype(F32)
            keep.append(jnp.where(first, total[:8], total[8:]))
            fin_s[:, STARTS[j] : STARTS[j] + WIDTHS[j]] = jnp.where(first, total[8:], total[:8])
        swap = remote(fin_s, fin_r, f_s, f_r, sibling)
        go(swap)
        for j in range(3):
            cols = pl.ds(pl.multiple_of(core * HALF + STARTS[j], 128), WIDTHS[j])
            out[:, cols] = (tok[:, cols].astype(F32) + keep[j]).astype(BF16)
        swap.wait_recv()
        out[:, rest_cols] = (tok[:, rest_cols].astype(F32) + fin_r[...]).astype(BF16)
        settle()

    wide = (608, tok.shape[1])
    pl.run_scoped(
        gather,
        pltpu.VMEM(wide, BF16),
        pltpu.VMEM(wide, BF16),
        pltpu.VMEM((4, 4, 4, 16, 608), F32),
        pltpu.VMEM((128, 608), F32),
    )
    pl.run_scoped(
        reduce,
        *(pltpu.VMEM((4, 4, 4, 16, w), BF16) for w in WIDTHS),
        *(pltpu.VMEM((2, 4, 16, w), F32) for w in WIDTHS),
    )


def per_device(
    tokens, route_ids, route_gain, norm_gain, dense_gate, dense_up, dense_down, expert_gate, expert_up, expert_down
):
    vmem = pl.BlockSpec(memory_space=pltpu.VMEM)
    hbm = pl.BlockSpec(memory_space=pl.ANY)
    dma = pltpu.SemaphoreType.DMA
    d, f = dense_gate.shape

    def sized(*lead):
        return [pltpu.VMEM((*lead, w), BF16) for w in WIDTHS]

    gathered = [pltpu.VMEM((2, 4, 4, 4, 16, w + (128 if j == 2 else 0)), BF16) for j, w in enumerate(WIDTHS)]
    return pl.pallas_call(
        block_kernel,
        out_shape=jax.ShapeDtypeStruct(tokens.shape, BF16),
        in_specs=[vmem] * 4 + [hbm] * 6,
        out_specs=vmem,
        scratch_shapes=gathered
        + [pltpu.VMEM((2, 8, HALF + 128), BF16), pltpu.VMEM((8, HALF + 128), BF16)]
        + [pltpu.VMEM((2 * f, HALF), BF16)] * 2
        + [pltpu.VMEM((4, 4, 4, 16, f), BF16)] * 2
        + [pltpu.VMEM((4, 4, 4, 16, 2 * f), BF16)]
        + [pltpu.VMEM((128, f), BF16)] * 2
        + [pltpu.VMEM((128, 2 * f), BF16), pltpu.VMEM((4, 4, 4, 16, 1), F32)]
        + sized(4, 2, 2, 16)
        + sized(4, 2, 4, 16)
        + sized(2, 2, 16)
        + sized(2, 4, 16)
        + sized(3, 16)
        + [pltpu.VMEM((8, HALF), F32)] * 2
        + [dma((6,)), dma((2,)), dma((2,)), dma, dma]
        + [dma((3, 3))] * 2
        + [dma((3, 4))] * 2
        + [dma((3, 4, 4))] * 4
        + [dma((4,)), dma((4,)), dma, dma]
        + [dma((3, 4, 4))] * 2
        + [dma((3, 4))] * 2
        + [dma((3, 3))] * 2
        + [dma, dma],
        compiler_params=pltpu.CompilerParams(
            collective_id=0, has_side_effects=True, vmem_limit_bytes=60 * 1024 * 1024
        ),
        name="gather_experts_sum",
    )(
        tokens, route_ids.T, route_gain.T, norm_gain.reshape(1, d),
        expert_gate.reshape(d, f).T, expert_up.reshape(d, f).T, dense_gate.T, dense_up.T,
        expert_down.reshape(f, d), dense_down,
    )


def solution(mesh):
    rows = P(("expert", "tensor"), None)
    return jax.shard_map(
        per_device,
        mesh=mesh,
        in_specs=(
            rows, rows, rows, P(),
            P(None, "tensor"), P(None, "tensor"), P("tensor", None),
            P("expert", None, "tensor"), P("expert", None, "tensor"), P("expert", "tensor", None),
        ),
        out_specs=rows,
        check_vma=False,
    )
```

```python
import jax
import jax.numpy as jnp
from jax import lax
from jax.experimental import pallas as pl
from jax.experimental.pallas import tpu as pltpu
from jax.sharding import PartitionSpec as P

F32, BF16 = jnp.float32, jnp.bfloat16
WIDTHS = (1280, 1152, 1152)
STARTS = (0, 1280, 2432)
HALF = 3584
GATHER = ((1, 2, 0), (2, 0, 1), (0, 1, 2))
REDUCE = ((0, 1, 2), (1, 2, 0), (2, 0, 1))
STEPS = (1, 3, 2)
LINES = (0, 3, 1, 2)
PLANES = (0, 3, 1, 2)
ALL = slice(None)


def position():
    e, t = lax.axis_index("expert"), lax.axis_index("tensor")
    x = lax.div(t, 8) * 2 + lax.div(e, 4)
    y = lax.rem(lax.div(t, 2), 4)
    z = lax.rem(e, 4)
    return (x, y, z), lax.rem(t, 2)


def device(pos, core):
    x, y, z = pos
    return (lax.rem(x, 2) * 4 + z, (lax.div(x, 2) * 4 + y) * 2 + core)


def moved(pos, axis, step):
    return tuple(lax.rem(p + step, 4) if a == axis else p for a, p in enumerate(pos))


def at(parts):
    return tuple(parts[a] for a in range(3))


def greet(pos, core):
    barrier = pltpu.get_barrier_semaphore()
    others = [device(moved(pos, a, s), c) for a in range(3) for s in STEPS for c in (core, 1 - core)]
    others.append(device(pos, 1 - core))
    for other in others:
        pl.semaphore_signal(barrier, inc=1, device_id=other, device_id_type=pl.DeviceIdType.MESH)
    return lambda: pl.semaphore_wait(barrier, len(others))


def remote(src, dst, send, recv, target):
    return pltpu.make_async_remote_copy(
        src_ref=src,
        dst_ref=dst,
        send_sem=send,
        recv_sem=recv,
        device_id=target,
        device_id_type=pl.DeviceIdType.MESH,
    )


def dot(a, b):
    return jnp.dot(a, b, preferred_element_type=F32)


def dot_t(a, b):
    return lax.dot_general(a, b, (((1,), (1,)), ((), ())), preferred_element_type=F32)


def block_kernel(
    tok, ids, gains, gain, wg_e, wu_e, wg_d, wu_d, wd_e, wd_d,
    out,
    x0, x1, x2, mine, other, n0, n1, n2,
    down_e, down_d, he, he_in, heb, hd, hd_in, hdb, weight,
    a0, a1, a2, b0, b1, b2, c0, c1, c2, d0, d1, d2, t0, t1, t2, u0, u1, u2,
    w_sem, down_s, down_r, pair_s, pair_r, g1s, g1r, g2s, g2r, g3s, g3r, fs, fr,
    he_s, he_r, hd_s, hd_r, s1, r1, s2, r2, s3, r3,
):
    xs = (x0, x1, x2)
    pos, core = position()
    rest = 1 - core
    sibling = device(pos, rest)
    own_cols = pl.ds(pl.multiple_of(core * HALF, 128), HALF)
    rest_cols = pl.ds(pl.multiple_of(rest * HALF, 128), HALF)
    x_low = lax.rem(pos[0], 2)
    first = core == 0
    lower, upper = slice(0, 2), slice(2, 4)
    sends = []

    def go(copy):
        copy.start()
        sends.append(copy)

    def settle():
        for copy in sends:
            copy.wait_send()
        sends.clear()

    def gather(up_e, up_d, acc, acc_d):
        top, low = pl.ds(0, 304), pl.ds(304, 304)
        loads = [
            pltpu.make_async_copy(src, dst, w_sem.at[i])
            for i, (src, dst) in enumerate((
                (wg_e, up_e.at[top]), (wu_e, up_e.at[low]), (wg_d, up_d.at[top]), (wu_d, up_d.at[low]),
                (wd_e.at[:, own_cols], down_e.at[top]), (wd_d.at[:, own_cols], down_d.at[top]),
            ))
        ]
        met = greet(pos, core)
        for load in loads:
            load.start()
        floats = tok[...].astype(F32)
        normed = floats * lax.rsqrt(jnp.mean(floats * floats, axis=1, keepdims=True) + 1e-05) * gain[...]
        lane = lax.broadcasted_iota(jnp.int32, (8, 128), 1).astype(F32)
        same = lax.broadcasted_iota(jnp.int32, (8, 8), 0) == lax.broadcasted_iota(jnp.int32, (8, 8), 1)
        extra = jnp.zeros((8, 128), F32)
        for k in range(2):
            g, who = (
                jnp.sum(jnp.where(same, ref[k : k + 1, :].astype(F32), 0.0), axis=1, keepdims=True)
                for ref in (gains, ids)
            )
            high = jnp.floor(g * (1.0 / 32.0))
            extra = extra + jnp.where(lane == who, high, 0.0)
            extra = extra + jnp.where(lane == who + 8.0, g - high * 32.0, 0.0)
        for h in range(2):
            mine[h, :, :HALF] = normed[:, h * HALF : (h + 1) * HALF].astype(BF16)
            mine[h, :, HALF:] = extra.astype(BF16)
        met()
        near = (n0, n1, n2)
        for j in range(3):
            span = slice(STARTS[j], STARTS[j] + xs[j].shape[-1])
            for k, d in enumerate(STEPS):
                there = moved(pos, GATHER[j][0], d)
                for i, half in enumerate((core, rest)):
                    target = device(there, half)
                    src = mine.at[half, :, span]
                    go(remote(src, near[j].at[k, core], g1s.at[j, k, i], g1r.at[j, k, core], target))
        swap = remote(mine.at[rest], other, pair_s, pair_r, sibling)
        go(swap)
        lends = [
            remote(src.at[:, rest_cols], dst.at[low], down_s.at[i], down_r.at[i], sibling)
            for i, (src, dst) in enumerate(((wd_e, down_e), (wd_d, down_d)))
        ]
        def copy(j, idx, sem_s, sem_r, target, half=None):
            ref = xs[j].at[(core if half is None else half, *idx)]
            return remote(ref, ref, sem_s, sem_r, target)

        for lend in lends:
            go(lend)
        acc[...] = jnp.zeros_like(acc)
        acc_d[...] = jnp.zeros_like(acc_d)

        sides = ((3, lower, 1), (1, upper, 3))

        def line(j, n, m, part=ALL):
            a1, a2, a3 = GATHER[j]
            return at({a1: part, a2: lax.rem(pos[a2] + LINES[n], 4), a3: lax.rem(pos[a3] + PLANES[m], 4)})

        def plane(j, m):
            a1, a2, a3 = GATHER[j]
            return at({a1: ALL, a2: ALL, a3: lax.rem(pos[a3] + PLANES[m], 4)})

        def forward(j, n, m):
            go(copy(j, line(j, n, m), fs.at[j, n, m], fr.at[j, n, m], sibling))

        def forwarded(m, lines=range(4)):
            for j in range(3):
                for n in lines:
                    copy(j, line(j, n, m), fs.at[j, n, m], fr.at[j, n, m], sibling, rest).wait_recv()

        def own(j, n):
            axis = GATHER[j][2]
            for k, d in enumerate((1, 3)):
                go(copy(j, line(j, n, 0), g3s.at[j, n, k], g3r.at[j, n, k], device(moved(pos, axis, d), core)))
            forward(j, n, 0)

        def relay(j, n):
            axis = GATHER[j][2]
            for k, (came, part, d) in enumerate(sides):
                m = 1 + k
                copy(j, line(j, n, m), g3s.at[j, n, k], g3r.at[j, n, k], sibling).wait_recv()
                target = device(moved(pos, axis, d), core)
                go(copy(j, line(j, n, m, part), g3s.at[j, n, 2 + k], g3r.at[j, n, 2 + k], target))
                forward(j, n, m)

        def add(j, idx, half):
            rows = xs[j][(half, *idx)].reshape(256, xs[j].shape[-1])[:, : WIDTHS[j]]
            span = pl.ds(pl.multiple_of(half * HALF + STARTS[j], 128), WIDTHS[j])
            acc[idx] += dot_t(rows, up_e[:, span]).reshape(4, 4, 16, 608)

        def add_dense(j):
            for h in range(2):
                rows = jnp.concatenate(
                    [
                        xs[j][h, x_low + 2 * k, :, pos[2]].reshape(64, xs[j].shape[-1])[:, : WIDTHS[j]]
                        for k in range(2)
                    ],
                    axis=0,
                )
                acc_d[...] += dot_t(rows, up_d[:, h * HALF + STARTS[j] : h * HALF + STARTS[j] + WIDTHS[j]])

        def add_lines(m, half, lines):
            for j in range(3):
                rows = jnp.concatenate(
                    [xs[j][(half, *line(j, n, m))].reshape(64, xs[j].shape[-1])[:, : WIDTHS[j]] for n in lines], axis=0
                )
                span = pl.ds(pl.multiple_of(half * HALF + STARTS[j], 128), WIDTHS[j])
                part = dot_t(rows, up_e[:, span])
                for i, n in enumerate(lines):
                    acc[line(j, n, m)] += part[i * 64 : i * 64 + 64].reshape(4, 16, 608)

        def adds(m, half):
            for j in range(3):
                add(j, plane(j, m), half)

        def stack(a, b):
            return jnp.concatenate([a.astype(F32), b.astype(F32)], axis=0).astype(BF16)

        swap.wait_recv()
        a, b = mine[core].astype(F32), other[...].astype(F32)
        slab = stack(jnp.where(first, a, b), jnp.where(first, b, a))
        for j in range(3):
            xs[j][(core, *pos)] = slab[:, STARTS[j] : STARTS[j] + xs[j].shape[-1]]
            for k, d in enumerate(STEPS):
                for c in range(2):
                    got = near[j].at[k, c]
                    remote(got, got, g1s.at[j, k, c], g1r.at[j, k, c], sibling).wait_recv()
                xs[j][(core, *moved(pos, GATHER[j][0], 4 - d))] = stack(near[j][k, 0], near[j][k, 1])
            axis = GATHER[j][1]
            for k, d in enumerate((1, 3)):
                go(copy(j, line(j, 0, 0), g2s.at[j, k], g2r.at[j, k], device(moved(pos, axis, d), core)))
            own(j, 0)
        for j in range(3):
            axis = GATHER[j][1]
            for k, (came, part, d) in enumerate(sides):
                n = 1 + k
                copy(j, line(j, n, 0), g2s.at[j, k], g2r.at[j, k], sibling).wait_recv()
                target = device(moved(pos, axis, d), core)
                go(copy(j, line(j, n, 0, part), g2s.at[j, 2 + k], g2r.at[j, 2 + k], target))
                own(j, n)
        for j in range(3):
            relay(j, 0)
        for j in range(3):
            for k, part in enumerate((lower, upper)):
                copy(j, line(j, 3, 0, part), g2s.at[j, 2 + k], g2r.at[j, 2 + k], sibling).wait_recv()
            own(j, 3)
        for load in loads:
            load.wait()
        for j in range(3):
            relay(j, 1)
            add(j, plane(j, 0), core)
        for j in range(3):
            relay(j, 2)
        forwarded(0)
        adds(0, rest)
        add_dense(2)
        for j in range(3):
            relay(j, 3)
        adds(1, core)
        adds(2, core)

        def last(n):
            for j in range(3):
                for k, part in enumerate((lower, upper)):
                    copy(j, line(j, n, 3, part), g3s.at[j, n, 2 + k], g3r.at[j, n, 2 + k], sibling).wait_recv()
                forward(j, n, 3)

        last(0)
        last(1)
        forwarded(1)
        adds(1, rest)
        last(2)
        forwarded(2)
        adds(2, rest)
        add_lines(3, core, (0, 1))
        forwarded(3, (0, 1))
        add_lines(3, rest, (0, 1))
        add_dense(0)
        last(3)
        add_lines(3, core, (2, 3))
        forwarded(3, (2, 3))
        add_lines(3, rest, (2, 3))

        def glu(v):
            g, u = v[:, :304], v[:, 304:]
            return (g / (1.0 + jnp.exp(-g)) * u).astype(BF16)

        e = lax.axis_index("expert")
        lanes = lax.broadcasted_iota(jnp.int32, (256, 128), 1)
        pick = jnp.where(lanes == e, 32.0, 0.0) + jnp.where(lanes == e + 8, 1.0, 0.0)
        trades = [remote(he.at[x], he_in.at[x], he_s.at[x], he_r.at[x], sibling) for x in range(4)]
        for x in range(4):
            he[x] = glu(acc[x].reshape(256, 608)).reshape(4, 4, 16, 304)
            go(trades[x])
        for x in range(4):
            pieces = x2[core, x, :, :, :, WIDTHS[2] :].reshape(256, 128).astype(F32)
            weight[x] = (jnp.sum(pieces * pick, axis=1, keepdims=True) * (1.0 / 1024.0)).reshape(4, 4, 16, 1)
        add_dense(1)
        hd[...] = glu(acc_d[...])
        go(remote(hd, hd_in, hd_s, hd_r, sibling))
        for x in range(4):
            trades[x].wait_recv()
            heb[x] = jnp.concatenate([he[x].reshape(256, 304), he_in[x].reshape(256, 304)], axis=1).reshape(4, 4, 16, 608)
        for lend in lends:
            lend.wait_recv()
        settle()

    def reduce(z0, z1, z2, q0, q1, q2):
        zs, dense = (z0, z1, z2), (q0, q1, q2)
        half1, full1, half2, full2, last_in = (a0, a1, a2), (b0, b1, b2), (c0, c1, c2), (d0, d1, d2), (t0, t1, t2)
        staged = (u0, u1, u2)

        def where(j, step):
            b1, b2, b3 = REDUCE[j]
            return at({b1: lax.rem(pos[b1] + step, 4), b2: ALL, b3: ALL})

        def produce(j, step):
            cols = slice(STARTS[j], STARTS[j] + WIDTHS[j])
            idx = where(j, step)
            part = dot(heb[idx].reshape(256, 608), down_e[:, cols]) * weight[idx].reshape(256, 1)
            zs[j][idx] = part.astype(BF16).reshape(4, 4, 16, WIDTHS[j])

        def produce_dense(j, step):
            idx = where(j, step)
            axis = REDUCE[j][0]
            places = []
            if axis == 0 and step % 2 == 0:
                places = [((idx[0], ALL, pos[2]), (lax.div(idx[0], 2), ALL))]
            elif axis == 1:
                places = [((x_low + 2 * k, idx[1], pos[2]), (k, idx[1])) for k in range(2)]
            elif axis == 2 and step == 0:
                places = [((x_low + 2 * k, ALL, pos[2]), (k, ALL)) for k in range(2)]
            for spot, src in places:
                zs[j][spot] = (zs[j][spot].astype(F32) + dense[j][src]).astype(BF16)

        def gain(j, idx, *others):
            total = zs[j][idx].astype(F32)
            for other in others:
                total = total + other[...].astype(F32)
            zs[j][idx] = total.astype(BF16)

        def row(j, step, r, part=ALL):
            b1, b2, b3 = REDUCE[j]
            return at({b1: lax.rem(pos[b1] + step, 4), b2: lax.rem(pos[b2] + r, 4), b3: part})

        def halves(j, step, r, axis, bufs, ss, rr):
            for k, (part, d) in enumerate(((lower, 1), (upper, 3))):
                go(remote(zs[j].at[row(j, step, r, part)], bufs.at[k], ss.at[k], rr.at[k], device(moved(pos, axis, d), core)))

        def whole(j, step, r, axis, k, bufs, fulls, ss, rr):
            part, d = ((lower, 1), (upper, 3))[k]
            remote(bufs.at[k], bufs.at[k], ss.at[k], rr.at[k], sibling).wait_recv()
            gain(j, row(j, step, r, part), bufs.at[k])
            go(remote(zs[j].at[row(j, step, r)], fulls.at[k], ss.at[2 + k], rr.at[2 + k], device(moved(pos, axis, d), core)))

        def close(j, r, fulls, ss, rr):
            for k in range(2):
                remote(fulls.at[k], fulls.at[k], ss.at[2 + k], rr.at[2 + k], sibling).wait_recv()
            gain(j, row(j, 0, r), fulls.at[0], fulls.at[1])

        def outer(j, n):
            return (half1[j].at[n], full1[j].at[n], s1.at[j, n], r1.at[j, n])

        def inner(j):
            return (half2[j], full2[j], s2.at[j], r2.at[j])

        order = (2, 1, 3, 0)
        def begin(j):
            for i, r in enumerate(order):
                bufs, _, ss, rr = outer(j, i)
                halves(j, 2, r, REDUCE[j][0], bufs, ss, rr)

        def go_on(j, i, k):
            bufs, fulls, ss, rr = outer(j, i)
            whole(j, order[1 + k], order[i], REDUCE[j][0], k, bufs, fulls, ss, rr)

        produce(2, 2)
        begin(2)
        remote(hd, hd_in, hd_s, hd_r, sibling).wait_recv()
        hdb[...] = jnp.concatenate([hd[...], hd_in[...]], axis=1)
        for j in range(3):
            part = dot(hdb[...], down_d[:, STARTS[j] : STARTS[j] + WIDTHS[j]])
            dense[j][...] = part.reshape(2, 4, 16, WIDTHS[j])
            if j < 2:
                produce(j, 2)
                produce_dense(j, 2)
                begin(j)
        for k in range(2):
            for j in range(3):
                produce(j, order[1 + k])
                produce_dense(j, order[1 + k])
            for i in range(3):
                for j in range(3):
                    go_on(j, i, k)
        for j in range(3):
            produce(j, 0)
            produce_dense(j, 0)
        for i, r in enumerate(order):
            if i == 2:
                for j in range(3):
                    for k in range(2):
                        go_on(j, 3, k)
            for j in range(3):
                _, fulls, ss, rr = outer(j, i)
                close(j, r, fulls, ss, rr)
                bufs, fulls, ss, rr = inner(j)
                if r == 2:
                    halves(j, 0, r, REDUCE[j][1], bufs, ss, rr)
                elif r:
                    whole(j, 0, r, REDUCE[j][1], i - 1, bufs, fulls, ss, rr)
        for j in range(3):
            _, fulls, ss, rr = inner(j)
            close(j, 0, fulls, ss, rr)
            for k, d in enumerate((*STEPS, 0)):
                there = moved(pos, REDUCE[j][2], d)
                rows = zs[j][there].astype(F32)
                for c in range(2):
                    staged[j][k, c] = rows[c * 8 : c * 8 + 8].astype(BF16)
                for i, c in enumerate((core, rest)):
                    if d or i:
                        src, dst = staged[j].at[k, c], last_in[j].at[k, core]
                        go(remote(src, dst, s3.at[j, k, i], r3.at[j, k, core], device(there, c)))
        for j in range(3):
            for i, half in enumerate((core, rest)):
                total = staged[j][3, core].astype(F32) if i == 0 else 0.0
                for k in range(3 + i):
                    got = last_in[j].at[k, half]
                    remote(got, got, s3.at[j, k, i], r3.at[j, k, half], sibling).wait_recv()
                    total = total + got[...].astype(F32)
                cols = pl.ds(pl.multiple_of(half * HALF + STARTS[j], 128), WIDTHS[j])
                out[:, cols] = (tok[:, cols].astype(F32) + total).astype(BF16)
        settle()

    wide = (608, tok.shape[1])
    pl.run_scoped(
        gather,
        pltpu.VMEM(wide, BF16),
        pltpu.VMEM(wide, BF16),
        pltpu.VMEM((4, 4, 4, 16, 608), F32),
        pltpu.VMEM((128, 608), F32),
    )
    pl.run_scoped(
        reduce,
        *(pltpu.VMEM((4, 4, 4, 16, w), BF16) for w in WIDTHS),
        *(pltpu.VMEM((2, 4, 16, w), F32) for w in WIDTHS),
    )


def per_device(
    tokens, route_ids, route_gain, norm_gain, dense_gate, dense_up, dense_down, expert_gate, expert_up, expert_down
):
    vmem = pl.BlockSpec(memory_space=pltpu.VMEM)
    hbm = pl.BlockSpec(memory_space=pl.ANY)
    dma = pltpu.SemaphoreType.DMA
    d, f = dense_gate.shape

    def sized(*lead):
        return [pltpu.VMEM((*lead, w), BF16) for w in WIDTHS]

    gathered = [pltpu.VMEM((2, 4, 4, 4, 16, w + (128 if j == 2 else 0)), BF16) for j, w in enumerate(WIDTHS)]
    return pl.pallas_call(
        block_kernel,
        out_shape=jax.ShapeDtypeStruct(tokens.shape, BF16),
        in_specs=[vmem] * 4 + [hbm] * 6,
        out_specs=vmem,
        scratch_shapes=gathered
        + [pltpu.VMEM((2, 8, HALF + 128), BF16), pltpu.VMEM((8, HALF + 128), BF16)]
        + [pltpu.VMEM((3, 2, 8, x.shape[-1]), BF16) for x in gathered]
        + [pltpu.VMEM((2 * f, HALF), BF16)] * 2
        + [pltpu.VMEM((4, 4, 4, 16, f), BF16)] * 2
        + [pltpu.VMEM((4, 4, 4, 16, 2 * f), BF16)]
        + [pltpu.VMEM((128, f), BF16)] * 2
        + [pltpu.VMEM((128, 2 * f), BF16), pltpu.VMEM((4, 4, 4, 16, 1), F32)]
        + sized(4, 2, 2, 16)
        + sized(4, 2, 4, 16)
        + sized(2, 2, 16)
        + sized(2, 4, 16)
        + sized(4, 2, 8)
        + sized(4, 2, 8)
        + [dma((6,)), dma((2,)), dma((2,)), dma, dma]
        + [dma((3, 3, 2))] * 2
        + [dma((3, 4))] * 2
        + [dma((3, 4, 4))] * 4
        + [dma((4,)), dma((4,)), dma, dma]
        + [dma((3, 4, 4))] * 2
        + [dma((3, 4))] * 2
        + [dma((3, 4, 2))] * 2,
        compiler_params=pltpu.CompilerParams(
            collective_id=0, has_side_effects=True, vmem_limit_bytes=60 * 1024 * 1024
        ),
        name="gather_experts_sum",
    )(
        tokens, route_ids.T, route_gain.T, norm_gain.reshape(1, d),
        expert_gate.reshape(d, f).T, expert_up.reshape(d, f).T, dense_gate.T, dense_up.T,
        expert_down.reshape(f, d), dense_down,
    )


def solution(mesh):
    rows = P(("expert", "tensor"), None)
    return jax.shard_map(
        per_device,
        mesh=mesh,
        in_specs=(
            rows, rows, rows, P(),
            P(None, "tensor"), P(None, "tensor"), P("tensor", None),
            P("expert", None, "tensor"), P("expert", None, "tensor"), P("expert", "tensor", None),
        ),
        out_specs=rows,
        check_vma=False,
    )
```

```python
import jax
import jax.numpy as jnp
from jax import lax
from jax.experimental import pallas as pl
from jax.experimental.pallas import tpu as pltpu
from jax.sharding import PartitionSpec as P

F32, BF16 = jnp.float32, jnp.bfloat16
WIDTHS = (1280, 1152, 1152)
STARTS = (0, 1280, 2432)
HALF = 3584
GATHER = ((1, 2, 0), (2, 0, 1), (0, 1, 2))
REDUCE = ((0, 1, 2), (1, 2, 0), (2, 0, 1))
STEPS = (1, 3, 2)
LINES = (0, 3, 1, 2)
PLANES = (0, 3, 1, 2)
ALL = slice(None)


def position():
    e, t = lax.axis_index("expert"), lax.axis_index("tensor")
    x = lax.div(t, 8) * 2 + lax.div(e, 4)
    y = lax.rem(lax.div(t, 2), 4)
    z = lax.rem(e, 4)
    return (x, y, z), lax.rem(t, 2)


def device(pos, core):
    x, y, z = pos
    return (lax.rem(x, 2) * 4 + z, (lax.div(x, 2) * 4 + y) * 2 + core)


def moved(pos, axis, step):
    return tuple(lax.rem(p + step, 4) if a == axis else p for a, p in enumerate(pos))


def at(parts):
    return tuple(parts[a] for a in range(3))


def greet(pos, core):
    barrier = pltpu.get_barrier_semaphore()
    others = [device(moved(pos, a, s), c) for a in range(3) for s in STEPS for c in (core, 1 - core)]
    others.append(device(pos, 1 - core))
    for other in others:
        pl.semaphore_signal(barrier, inc=1, device_id=other, device_id_type=pl.DeviceIdType.MESH)
    return lambda: pl.semaphore_wait(barrier, len(others))


def remote(src, dst, send, recv, target):
    return pltpu.make_async_remote_copy(
        src_ref=src,
        dst_ref=dst,
        send_sem=send,
        recv_sem=recv,
        device_id=target,
        device_id_type=pl.DeviceIdType.MESH,
    )


def dot(a, b):
    return jnp.dot(a, b, preferred_element_type=F32)


def dot_t(a, b):
    return lax.dot_general(a, b, (((1,), (1,)), ((), ())), preferred_element_type=F32)


def block_kernel(
    tok, ids, gains, gain, wg_e, wu_e, wg_d, wu_d, wd_e, wd_d,
    out,
    x0, x1, x2, mine, other, n0, n1, n2,
    down_e, down_d, he, he_in, heb, hd, hd_in, hdb, weight,
    a0, a1, a2, b0, b1, b2, c0, c1, c2, d0, d1, d2, t0, t1, t2, u0, u1, u2,
    w_sem, down_s, down_r, pair_s, pair_r, g1s, g1r, g2s, g2r, g3s, g3r, fs, fr,
    he_s, he_r, hd_s, hd_r, s1, r1, s2, r2, s3, r3,
):
    xs = (x0, x1, x2)
    pos, core = position()
    rest = 1 - core
    sibling = device(pos, rest)
    own_cols = pl.ds(pl.multiple_of(core * HALF, 128), HALF)
    rest_cols = pl.ds(pl.multiple_of(rest * HALF, 128), HALF)
    dense_x = (pos[0], 3 - pos[0])
    first = core == 0
    lower, upper = slice(0, 2), slice(2, 4)
    sends = []

    def go(copy):
        copy.start()
        sends.append(copy)

    def settle():
        for copy in sends:
            copy.wait_send()
        sends.clear()

    trades = [remote(he.at[x], he_in.at[x], he_s.at[x], he_r.at[x], sibling) for x in range(4)]
    trade = remote(hd, hd_in, hd_s, hd_r, sibling)

    def gather(up_e, up_d, acc, acc_d):
        top, low = pl.ds(0, 304), pl.ds(304, 304)
        loads = [
            pltpu.make_async_copy(src, dst, w_sem.at[i])
            for i, (src, dst) in enumerate((
                (wg_e, up_e.at[top]), (wu_e, up_e.at[low]), (wg_d, up_d.at[top]), (wu_d, up_d.at[low]),
                (wd_e.at[:, own_cols], down_e.at[top]), (wd_d.at[:, own_cols], down_d.at[top]),
            ))
        ]
        met = greet(pos, core)
        for load in loads:
            load.start()
        floats = tok[...].astype(F32)
        normed = floats * lax.rsqrt(jnp.mean(floats * floats, axis=1, keepdims=True) + 1e-05) * gain[...]
        lane = lax.broadcasted_iota(jnp.int32, (8, 128), 1).astype(F32)
        same = lax.broadcasted_iota(jnp.int32, (8, 8), 0) == lax.broadcasted_iota(jnp.int32, (8, 8), 1)
        extra = jnp.zeros((8, 128), F32)
        for k in range(2):
            g, who = (
                jnp.sum(jnp.where(same, ref[k : k + 1, :].astype(F32), 0.0), axis=1, keepdims=True)
                for ref in (gains, ids)
            )
            high = jnp.floor(g * (1.0 / 32.0))
            extra = extra + jnp.where(lane == who, high, 0.0)
            extra = extra + jnp.where(lane == who + 8.0, g - high * 32.0, 0.0)
        for h in range(2):
            mine[h, :, :HALF] = normed[:, h * HALF : (h + 1) * HALF].astype(BF16)
            mine[h, :, HALF:] = extra.astype(BF16)
        met()
        near = (n0, n1, n2)
        for j in range(3):
            span = slice(STARTS[j], STARTS[j] + xs[j].shape[-1])
            for k, d in enumerate(STEPS):
                there = moved(pos, GATHER[j][0], d)
                for i, half in enumerate((core, rest)):
                    target = device(there, half)
                    src = mine.at[half, :, span]
                    go(remote(src, near[j].at[k, core], g1s.at[j, k, i], g1r.at[j, k, core], target))
        swap = remote(mine.at[rest], other, pair_s, pair_r, sibling)
        go(swap)
        lends = [
            remote(src.at[:, rest_cols], dst.at[low], down_s.at[i], down_r.at[i], sibling)
            for i, (src, dst) in enumerate(((wd_e, down_e), (wd_d, down_d)))
        ]
        def copy(j, idx, sem_s, sem_r, target, half=None):
            ref = xs[j].at[(core if half is None else half, *idx)]
            return remote(ref, ref, sem_s, sem_r, target)

        for lend in lends:
            go(lend)
        acc[...] = jnp.zeros_like(acc)
        acc_d[...] = jnp.zeros_like(acc_d)

        sides = ((3, lower, 1), (1, upper, 3))

        def line(j, n, m, part=ALL):
            a1, a2, a3 = GATHER[j]
            return at({a1: part, a2: lax.rem(pos[a2] + LINES[n], 4), a3: lax.rem(pos[a3] + PLANES[m], 4)})

        def plane(j, m):
            a1, a2, a3 = GATHER[j]
            return at({a1: ALL, a2: ALL, a3: lax.rem(pos[a3] + PLANES[m], 4)})

        def forward(j, n, m):
            go(copy(j, line(j, n, m), fs.at[j, n, m], fr.at[j, n, m], sibling))

        def forwarded(m, lines=range(4)):
            for j in range(3):
                for n in lines:
                    copy(j, line(j, n, m), fs.at[j, n, m], fr.at[j, n, m], sibling, rest).wait_recv()

        def own(j, n):
            axis = GATHER[j][2]
            for k, d in enumerate((1, 3)):
                go(copy(j, line(j, n, 0), g3s.at[j, n, k], g3r.at[j, n, k], device(moved(pos, axis, d), core)))
            forward(j, n, 0)

        def relay(j, n):
            axis = GATHER[j][2]
            for k, (came, part, d) in enumerate(sides):
                m = 1 + k
                copy(j, line(j, n, m), g3s.at[j, n, k], g3r.at[j, n, k], sibling).wait_recv()
                target = device(moved(pos, axis, d), core)
                go(copy(j, line(j, n, m, part), g3s.at[j, n, 2 + k], g3r.at[j, n, 2 + k], target))
                forward(j, n, m)

        def add(j, idx, half):
            rows = xs[j][(half, *idx)].reshape(256, xs[j].shape[-1])[:, : WIDTHS[j]]
            span = pl.ds(pl.multiple_of(half * HALF + STARTS[j], 128), WIDTHS[j])
            acc[idx] += dot_t(rows, up_e[:, span]).reshape(4, 4, 16, 608)

        def add_dense(j):
            for h in range(2):
                rows = jnp.concatenate(
                    [
                        xs[j][h, dense_x[k], :, pos[2]].reshape(64, xs[j].shape[-1])[:, : WIDTHS[j]]
                        for k in range(2)
                    ],
                    axis=0,
                )
                acc_d[...] += dot_t(rows, up_d[:, h * HALF + STARTS[j] : h * HALF + STARTS[j] + WIDTHS[j]])

        def add_lines(m, half, lines):
            for j in range(3):
                rows = jnp.concatenate(
                    [xs[j][(half, *line(j, n, m))].reshape(64, xs[j].shape[-1])[:, : WIDTHS[j]] for n in lines], axis=0
                )
                span = pl.ds(pl.multiple_of(half * HALF + STARTS[j], 128), WIDTHS[j])
                part = dot_t(rows, up_e[:, span])
                for i, n in enumerate(lines):
                    acc[line(j, n, m)] += part[i * 64 : i * 64 + 64].reshape(4, 16, 608)

        def adds(m, half):
            for j in range(3):
                add(j, plane(j, m), half)

        def stack(a, b):
            return jnp.concatenate([a.astype(F32), b.astype(F32)], axis=0).astype(BF16)

        swap.wait_recv()
        a, b = mine[core].astype(F32), other[...].astype(F32)
        slab = stack(jnp.where(first, a, b), jnp.where(first, b, a))
        for j in range(3):
            xs[j][(core, *pos)] = slab[:, STARTS[j] : STARTS[j] + xs[j].shape[-1]]
            for k, d in enumerate(STEPS):
                for c in range(2):
                    got = near[j].at[k, c]
                    remote(got, got, g1s.at[j, k, c], g1r.at[j, k, c], sibling).wait_recv()
                xs[j][(core, *moved(pos, GATHER[j][0], 4 - d))] = stack(near[j][k, 0], near[j][k, 1])
            axis = GATHER[j][1]
            for k, d in enumerate((1, 3)):
                go(copy(j, line(j, 0, 0), g2s.at[j, k], g2r.at[j, k], device(moved(pos, axis, d), core)))
            own(j, 0)
        for j in range(3):
            axis = GATHER[j][1]
            for k, (came, part, d) in enumerate(sides):
                n = 1 + k
                copy(j, line(j, n, 0), g2s.at[j, k], g2r.at[j, k], sibling).wait_recv()
                target = device(moved(pos, axis, d), core)
                go(copy(j, line(j, n, 0, part), g2s.at[j, 2 + k], g2r.at[j, 2 + k], target))
            own(j, 1)
        for j in range(3):
            relay(j, 0)
            own(j, 2)
        for j in range(3):
            for k, part in enumerate((lower, upper)):
                copy(j, line(j, 3, 0, part), g2s.at[j, 2 + k], g2r.at[j, 2 + k], sibling).wait_recv()
            own(j, 3)
        for load in loads:
            load.wait()
        for j in range(3):
            relay(j, 1)
            add(j, plane(j, 0), core)
        for j in range(3):
            relay(j, 2)
        forwarded(0)
        adds(0, rest)
        add_dense(2)
        for j in range(3):
            relay(j, 3)
        adds(1, core)
        adds(2, core)

        def last(n):
            for j in range(3):
                for k, part in enumerate((lower, upper)):
                    copy(j, line(j, n, 3, part), g3s.at[j, n, 2 + k], g3r.at[j, n, 2 + k], sibling).wait_recv()
                forward(j, n, 3)

        last(0)
        last(1)
        forwarded(1)
        adds(1, rest)
        last(2)
        forwarded(2)
        adds(2, rest)
        def glu(v):
            g, u = v[:, :304], v[:, 304:]
            return (g / (1.0 + jnp.exp(-g)) * u).astype(BF16)

        add_lines(3, core, (0, 1))
        forwarded(3, (0, 1))
        add_lines(3, rest, (0, 1))
        add_dense(0)
        forwarded(3, (2,))
        add_dense(1)
        hd[...] = glu(acc_d[...])
        trade.start()
        last(3)
        add_lines(3, core, (2, 3))
        forwarded(3, (3,))
        add_lines(3, rest, (2, 3))

        e = lax.axis_index("expert")
        lanes = lax.broadcasted_iota(jnp.int32, (256, 128), 1)
        pick = jnp.where(lanes == e, 32.0, 0.0) + jnp.where(lanes == e + 8, 1.0, 0.0)
        for x in range(4):
            he[x] = glu(acc[x].reshape(256, 608)).reshape(4, 4, 16, 304)
            trades[x].start()
        for x in range(4):
            pieces = x2[core, x, :, :, :, WIDTHS[2] :].reshape(256, 128).astype(F32)
            weight[x] = (jnp.sum(pieces * pick, axis=1, keepdims=True) * (1.0 / 1024.0)).reshape(4, 4, 16, 1)
        for lend in lends:
            lend.wait_recv()
        settle()

    def reduce(z0, z1, z2, q0, q1, q2):
        zs, dense = (z0, z1, z2), (q0, q1, q2)
        half1, full1, half2, full2, last_in = (a0, a1, a2), (b0, b1, b2), (c0, c1, c2), (d0, d1, d2), (t0, t1, t2)
        staged = (u0, u1, u2)

        def where(j, step):
            b1, b2, b3 = REDUCE[j]
            return at({b1: lax.rem(pos[b1] + step, 4), b2: ALL, b3: ALL})

        def produce(j, step):
            cols = slice(STARTS[j], STARTS[j] + WIDTHS[j])
            idx = where(j, step)
            part = dot(heb[idx].reshape(256, 608), down_e[:, cols]) * weight[idx].reshape(256, 1)
            zs[j][idx] = part.astype(BF16).reshape(4, 4, 16, WIDTHS[j])

        def produce_dense(j, step):
            idx = where(j, step)
            axis = REDUCE[j][0]
            places = []
            if axis == 0 and step == 0:
                places = [((idx[0], ALL, pos[2]), (0, ALL))]
            elif axis == 1:
                places = [((dense_x[k], idx[1], pos[2]), (k, idx[1])) for k in range(2)]
            elif axis == 2 and step == 0:
                places = [((dense_x[k], ALL, pos[2]), (k, ALL)) for k in range(2)]
            elif axis == 0 and step % 2:

                @pl.when(idx[0] == dense_x[1])
                def _():
                    spot = (idx[0], ALL, pos[2])
                    zs[j][spot] = (zs[j][spot].astype(F32) + dense[j][1]).astype(BF16)

            for spot, src in places:
                zs[j][spot] = (zs[j][spot].astype(F32) + dense[j][src]).astype(BF16)

        def gain(j, idx, *others):
            total = zs[j][idx].astype(F32)
            for other in others:
                total = total + other[...].astype(F32)
            zs[j][idx] = total.astype(BF16)

        def row(j, step, r, part=ALL):
            b1, b2, b3 = REDUCE[j]
            return at({b1: lax.rem(pos[b1] + step, 4), b2: lax.rem(pos[b2] + r, 4), b3: part})

        def halves(j, step, r, axis, bufs, ss, rr):
            for k, (part, d) in enumerate(((lower, 1), (upper, 3))):
                go(remote(zs[j].at[row(j, step, r, part)], bufs.at[k], ss.at[k], rr.at[k], device(moved(pos, axis, d), core)))

        def whole(j, step, r, axis, k, bufs, fulls, ss, rr):
            part, d = ((lower, 1), (upper, 3))[k]
            remote(bufs.at[k], bufs.at[k], ss.at[k], rr.at[k], sibling).wait_recv()
            gain(j, row(j, step, r, part), bufs.at[k])
            go(remote(zs[j].at[row(j, step, r)], fulls.at[k], ss.at[2 + k], rr.at[2 + k], device(moved(pos, axis, d), core)))

        def close(j, r, fulls, ss, rr):
            for k in range(2):
                remote(fulls.at[k], fulls.at[k], ss.at[2 + k], rr.at[2 + k], sibling).wait_recv()
            gain(j, row(j, 0, r), fulls.at[0], fulls.at[1])

        def outer(j, n):
            return (half1[j].at[n], full1[j].at[n], s1.at[j, n], r1.at[j, n])

        def inner(j):
            return (half2[j], full2[j], s2.at[j], r2.at[j])

        order = (2, 1, 3, 0)
        def begin(j, i):
            bufs, _, ss, rr = outer(j, i)
            halves(j, 2, order[i], REDUCE[j][0], bufs, ss, rr)

        def go_on(j, i, k):
            bufs, fulls, ss, rr = outer(j, i)
            whole(j, order[1 + k], order[i], REDUCE[j][0], k, bufs, fulls, ss, rr)

        trade.wait_recv()
        hdb[...] = jnp.concatenate([hd[...], hd_in[...]], axis=1)
        for j in range(3):
            part = dot(hdb[...], down_d[:, STARTS[j] : STARTS[j] + WIDTHS[j]])
            dense[j][...] = part.reshape(2, 4, 16, WIDTHS[j])
        for x in range(4):
            trades[x].wait_recv()
            heb[x] = jnp.concatenate([he[x].reshape(256, 304), he_in[x].reshape(256, 304)], axis=1).reshape(4, 4, 16, 608)
        for j in range(3):
            produce(j, 2)
            produce_dense(j, 2)
            begin(j, 0)
        def next_line(i):
            for j in range(3):
                for k in range(2):
                    go_on(j, i, k)

        for k in range(2):
            for j in range(3):
                produce(j, order[1 + k])
                produce_dense(j, order[1 + k])
                begin(j, 1 + k)
        next_line(0)
        for j in range(3):
            begin(j, 3)
        next_line(1)
        for j in range(3):
            produce(j, 0)
            produce_dense(j, 0)
        for i, r in enumerate(order):
            if i in (1, 2):
                next_line(i + 1)
            for j in range(3):
                _, fulls, ss, rr = outer(j, i)
                close(j, r, fulls, ss, rr)
                bufs, fulls, ss, rr = inner(j)
                if r == 2:
                    halves(j, 0, r, REDUCE[j][1], bufs, ss, rr)
                elif r:
                    whole(j, 0, r, REDUCE[j][1], i - 1, bufs, fulls, ss, rr)
        for j in range(3):
            _, fulls, ss, rr = inner(j)
            close(j, 0, fulls, ss, rr)
            for k, d in enumerate((*STEPS, 0)):
                there = moved(pos, REDUCE[j][2], d)
                rows = zs[j][there].astype(F32)
                for c in range(2):
                    staged[j][k, c] = rows[c * 8 : c * 8 + 8].astype(BF16)
                for i, c in enumerate((core, rest)):
                    if d or i:
                        src, dst = staged[j].at[k, c], last_in[j].at[k, core]
                        go(remote(src, dst, s3.at[j, k, i], r3.at[j, k, core], device(there, c)))
        for j in range(3):
            for i, half in enumerate((core, rest)):
                total = staged[j][3, core].astype(F32) if i == 0 else 0.0
                for k in range(3 + i):
                    got = last_in[j].at[k, half]
                    remote(got, got, s3.at[j, k, i], r3.at[j, k, half], sibling).wait_recv()
                    total = total + got[...].astype(F32)
                cols = pl.ds(pl.multiple_of(half * HALF + STARTS[j], 128), WIDTHS[j])
                out[:, cols] = (tok[:, cols].astype(F32) + total).astype(BF16)
        for copy in (*trades, trade):
            copy.wait_send()
        settle()

    wide = (608, tok.shape[1])
    pl.run_scoped(
        gather,
        pltpu.VMEM(wide, BF16),
        pltpu.VMEM(wide, BF16),
        pltpu.VMEM((4, 4, 4, 16, 608), F32),
        pltpu.VMEM((128, 608), F32),
    )
    pl.run_scoped(
        reduce,
        *(pltpu.VMEM((4, 4, 4, 16, w), BF16) for w in WIDTHS),
        *(pltpu.VMEM((2, 4, 16, w), F32) for w in WIDTHS),
    )


def per_device(
    tokens, route_ids, route_gain, norm_gain, dense_gate, dense_up, dense_down, expert_gate, expert_up, expert_down
):
    vmem = pl.BlockSpec(memory_space=pltpu.VMEM)
    hbm = pl.BlockSpec(memory_space=pl.ANY)
    dma = pltpu.SemaphoreType.DMA
    d, f = dense_gate.shape

    def sized(*lead):
        return [pltpu.VMEM((*lead, w), BF16) for w in WIDTHS]

    gathered = [pltpu.VMEM((2, 4, 4, 4, 16, w + (128 if j == 2 else 0)), BF16) for j, w in enumerate(WIDTHS)]
    return pl.pallas_call(
        block_kernel,
        out_shape=jax.ShapeDtypeStruct(tokens.shape, BF16),
        in_specs=[vmem] * 4 + [hbm] * 6,
        out_specs=vmem,
        scratch_shapes=gathered
        + [pltpu.VMEM((2, 8, HALF + 128), BF16), pltpu.VMEM((8, HALF + 128), BF16)]
        + [pltpu.VMEM((3, 2, 8, x.shape[-1]), BF16) for x in gathered]
        + [pltpu.VMEM((2 * f, HALF), BF16)] * 2
        + [pltpu.VMEM((4, 4, 4, 16, f), BF16)] * 2
        + [pltpu.VMEM((4, 4, 4, 16, 2 * f), BF16)]
        + [pltpu.VMEM((128, f), BF16)] * 2
        + [pltpu.VMEM((128, 2 * f), BF16), pltpu.VMEM((4, 4, 4, 16, 1), F32)]
        + sized(4, 2, 2, 16)
        + sized(4, 2, 4, 16)
        + sized(2, 2, 16)
        + sized(2, 4, 16)
        + sized(4, 2, 8)
        + sized(4, 2, 8)
        + [dma((6,)), dma((2,)), dma((2,)), dma, dma]
        + [dma((3, 3, 2))] * 2
        + [dma((3, 4))] * 2
        + [dma((3, 4, 4))] * 4
        + [dma((4,)), dma((4,)), dma, dma]
        + [dma((3, 4, 4))] * 2
        + [dma((3, 4))] * 2
        + [dma((3, 4, 2))] * 2,
        compiler_params=pltpu.CompilerParams(
            collective_id=0, has_side_effects=True, vmem_limit_bytes=60 * 1024 * 1024
        ),
        name="gather_experts_sum",
    )(
        tokens, route_ids.T, route_gain.T, norm_gain.reshape(1, d),
        expert_gate.reshape(d, f).T, expert_up.reshape(d, f).T, dense_gate.T, dense_up.T,
        expert_down.reshape(f, d), dense_down,
    )


def solution(mesh):
    rows = P(("expert", "tensor"), None)
    return jax.shard_map(
        per_device,
        mesh=mesh,
        in_specs=(
            rows, rows, rows, P(),
            P(None, "tensor"), P(None, "tensor"), P("tensor", None),
            P("expert", None, "tensor"), P("expert", None, "tensor"), P("expert", "tensor", None),
        ),
        out_specs=rows,
        check_vma=False,
    )
```

```python
import jax
import jax.numpy as jnp
from jax import lax
from jax.experimental import pallas as pl
from jax.experimental.pallas import tpu as pltpu
from jax.sharding import PartitionSpec as P

F32, BF16 = jnp.float32, jnp.bfloat16
WIDTHS = (1280, 1152, 1152)
STARTS = (0, 1280, 2432)
HALF = 3584
GATHER = ((1, 2, 0), (2, 0, 1), (0, 1, 2))
REDUCE = ((0, 1, 2), (1, 2, 0), (2, 0, 1))
STEPS = (1, 3, 2)
LINES = (0, 3, 1, 2)
PLANES = (0, 3, 1, 2)
ALL = slice(None)


def position():
    e, t = lax.axis_index("expert"), lax.axis_index("tensor")
    x = lax.div(t, 8) * 2 + lax.div(e, 4)
    y = lax.rem(lax.div(t, 2), 4)
    z = lax.rem(e, 4)
    return (x, y, z), lax.rem(t, 2)


def device(pos, core):
    x, y, z = pos
    return (lax.rem(x, 2) * 4 + z, (lax.div(x, 2) * 4 + y) * 2 + core)


def moved(pos, axis, step):
    return tuple(lax.rem(p + step, 4) if a == axis else p for a, p in enumerate(pos))


def at(parts):
    return tuple(parts[a] for a in range(3))


def greet(pos, core):
    barrier = pltpu.get_barrier_semaphore()
    others = [device(moved(pos, a, s), c) for a in range(3) for s in STEPS for c in (core, 1 - core)]
    others.append(device(pos, 1 - core))
    for other in others:
        pl.semaphore_signal(barrier, inc=1, device_id=other, device_id_type=pl.DeviceIdType.MESH)
    return lambda: pl.semaphore_wait(barrier, len(others))


def remote(src, dst, send, recv, target):
    return pltpu.make_async_remote_copy(
        src_ref=src,
        dst_ref=dst,
        send_sem=send,
        recv_sem=recv,
        device_id=target,
        device_id_type=pl.DeviceIdType.MESH,
    )


def dot(a, b):
    return jnp.dot(a, b, preferred_element_type=F32)


def dot_t(a, b):
    return lax.dot_general(a, b, (((1,), (1,)), ((), ())), preferred_element_type=F32)


def block_kernel(
    tok, ids, gains, gain, wg_e, wu_e, wg_d, wu_d, wd_e, wd_d,
    out,
    x0, x1, x2, mine, other, n0, n1, n2,
    down_e, down_d, he, he_in, heb, hd, hd_in, hdb, weight,
    a0, a1, a2, b0, b1, b2, c0, c1, c2, d0, d1, d2, t0, t1, t2, u0, u1, u2,
    w_sem, down_s, down_r, pair_s, pair_r, g1s, g1r, g2s, g2r, g3s, g3r, fs, fr,
    he_s, he_r, hd_s, hd_r, s1, r1, s2, r2, s3, r3,
):
    xs = (x0, x1, x2)
    pos, core = position()
    rest = 1 - core
    sibling = device(pos, rest)
    own_cols = pl.ds(pl.multiple_of(core * HALF, 128), HALF)
    rest_cols = pl.ds(pl.multiple_of(rest * HALF, 128), HALF)
    dense_x = (pos[0], 3 - pos[0])
    first = core == 0
    lower, upper = slice(0, 2), slice(2, 4)
    sends = []

    def go(copy):
        copy.start()
        sends.append(copy)

    def settle():
        for copy in sends:
            copy.wait_send()
        sends.clear()

    trades = [remote(he.at[x], he_in.at[x], he_s.at[x], he_r.at[x], sibling) for x in range(4)]
    trade = remote(hd, hd_in, hd_s, hd_r, sibling)

    def gather(up_e, up_d, acc, acc_d):
        top, low = pl.ds(0, 304), pl.ds(304, 304)
        loads = [
            pltpu.make_async_copy(src, dst, w_sem.at[i])
            for i, (src, dst) in enumerate((
                (wg_e, up_e.at[top]), (wu_e, up_e.at[low]), (wg_d, up_d.at[top]), (wu_d, up_d.at[low]),
                (wd_e.at[:, own_cols], down_e.at[top]), (wd_d.at[:, own_cols], down_d.at[top]),
            ))
        ]
        met = greet(pos, core)
        for load in loads:
            load.start()
        floats = tok[...].astype(F32)
        normed = floats * lax.rsqrt(jnp.mean(floats * floats, axis=1, keepdims=True) + 1e-05) * gain[...]
        lane = lax.broadcasted_iota(jnp.int32, (8, 128), 1).astype(F32)
        same = lax.broadcasted_iota(jnp.int32, (8, 8), 0) == lax.broadcasted_iota(jnp.int32, (8, 8), 1)
        extra = jnp.zeros((8, 128), F32)
        for k in range(2):
            g, who = (
                jnp.sum(jnp.where(same, ref[k : k + 1, :].astype(F32), 0.0), axis=1, keepdims=True)
                for ref in (gains, ids)
            )
            high = jnp.floor(g * (1.0 / 32.0))
            extra = extra + jnp.where(lane == who, high, 0.0)
            extra = extra + jnp.where(lane == who + 8.0, g - high * 32.0, 0.0)
        for h in range(2):
            mine[h, :, :HALF] = normed[:, h * HALF : (h + 1) * HALF].astype(BF16)
            mine[h, :, HALF:] = extra.astype(BF16)
        met()
        near = (n0, n1, n2)
        for j in range(3):
            span = slice(STARTS[j], STARTS[j] + xs[j].shape[-1])
            for k, d in enumerate(STEPS):
                there = moved(pos, GATHER[j][0], d)
                for i, half in enumerate((core, rest)):
                    target = device(there, half)
                    src = mine.at[half, :, span]
                    go(remote(src, near[j].at[k, core], g1s.at[j, k, i], g1r.at[j, k, core], target))
        swap = remote(mine.at[rest], other, pair_s, pair_r, sibling)
        go(swap)
        lends = [
            remote(src.at[:, rest_cols], dst.at[low], down_s.at[i], down_r.at[i], sibling)
            for i, (src, dst) in enumerate(((wd_e, down_e), (wd_d, down_d)))
        ]
        def copy(j, idx, sem_s, sem_r, target, half=None):
            ref = xs[j].at[(core if half is None else half, *idx)]
            return remote(ref, ref, sem_s, sem_r, target)

        for lend in lends:
            go(lend)
        acc[...] = jnp.zeros_like(acc)
        acc_d[...] = jnp.zeros_like(acc_d)

        sides = ((3, lower, 1), (1, upper, 3))

        def line(j, n, m, part=ALL):
            a1, a2, a3 = GATHER[j]
            return at({a1: part, a2: lax.rem(pos[a2] + LINES[n], 4), a3: lax.rem(pos[a3] + PLANES[m], 4)})

        def plane(j, m):
            a1, a2, a3 = GATHER[j]
            return at({a1: ALL, a2: ALL, a3: lax.rem(pos[a3] + PLANES[m], 4)})

        def forward(j, n, m):
            go(copy(j, line(j, n, m), fs.at[j, n, m], fr.at[j, n, m], sibling))

        def forwarded(m, lines=range(4)):
            for j in range(3):
                for n in lines:
                    copy(j, line(j, n, m), fs.at[j, n, m], fr.at[j, n, m], sibling, rest).wait_recv()

        def own(j, n):
            axis = GATHER[j][2]
            for k, d in enumerate((1, 3)):
                go(copy(j, line(j, n, 0), g3s.at[j, n, k], g3r.at[j, n, k], device(moved(pos, axis, d), core)))
            forward(j, n, 0)

        def relay(j, n):
            axis = GATHER[j][2]
            for k, (came, part, d) in enumerate(sides):
                m = 1 + k
                copy(j, line(j, n, m), g3s.at[j, n, k], g3r.at[j, n, k], sibling).wait_recv()
                target = device(moved(pos, axis, d), core)
                go(copy(j, line(j, n, m, part), g3s.at[j, n, 2 + k], g3r.at[j, n, 2 + k], target))
                forward(j, n, m)

        def add(j, idx, half):
            rows = xs[j][(half, *idx)].reshape(256, xs[j].shape[-1])[:, : WIDTHS[j]]
            span = pl.ds(pl.multiple_of(half * HALF + STARTS[j], 128), WIDTHS[j])
            acc[idx] += dot_t(rows, up_e[:, span]).reshape(4, 4, 16, 608)

        def add_dense(j):
            for h in range(2):
                rows = jnp.concatenate(
                    [
                        xs[j][h, dense_x[k], :, pos[2]].reshape(64, xs[j].shape[-1])[:, : WIDTHS[j]]
                        for k in range(2)
                    ],
                    axis=0,
                )
                acc_d[...] += dot_t(rows, up_d[:, h * HALF + STARTS[j] : h * HALF + STARTS[j] + WIDTHS[j]])

        def add_lines(m, half, lines):
            for j in range(3):
                rows = jnp.concatenate(
                    [xs[j][(half, *line(j, n, m))].reshape(64, xs[j].shape[-1])[:, : WIDTHS[j]] for n in lines], axis=0
                )
                span = pl.ds(pl.multiple_of(half * HALF + STARTS[j], 128), WIDTHS[j])
                part = dot_t(rows, up_e[:, span])
                for i, n in enumerate(lines):
                    acc[line(j, n, m)] += part[i * 64 : i * 64 + 64].reshape(4, 16, 608)

        def adds(m, half):
            for j in range(3):
                add(j, plane(j, m), half)

        def stack(a, b):
            return jnp.concatenate([a.astype(F32), b.astype(F32)], axis=0).astype(BF16)

        swap.wait_recv()
        a, b = mine[core].astype(F32), other[...].astype(F32)
        slab = stack(jnp.where(first, a, b), jnp.where(first, b, a))
        for j in range(3):
            xs[j][(core, *pos)] = slab[:, STARTS[j] : STARTS[j] + xs[j].shape[-1]]
            for k, d in enumerate(STEPS):
                for c in range(2):
                    got = near[j].at[k, c]
                    remote(got, got, g1s.at[j, k, c], g1r.at[j, k, c], sibling).wait_recv()
                xs[j][(core, *moved(pos, GATHER[j][0], 4 - d))] = stack(near[j][k, 0], near[j][k, 1])
            axis = GATHER[j][1]
            for k, d in enumerate((1, 3)):
                go(copy(j, line(j, 0, 0), g2s.at[j, k], g2r.at[j, k], device(moved(pos, axis, d), core)))
            own(j, 0)
        for j in range(3):
            axis = GATHER[j][1]
            for k, (came, part, d) in enumerate(sides):
                n = 1 + k
                copy(j, line(j, n, 0), g2s.at[j, k], g2r.at[j, k], sibling).wait_recv()
                target = device(moved(pos, axis, d), core)
                go(copy(j, line(j, n, 0, part), g2s.at[j, 2 + k], g2r.at[j, 2 + k], target))
            own(j, 1)
        for j in range(3):
            relay(j, 0)
            own(j, 2)
        for j in range(3):
            for k, part in enumerate((lower, upper)):
                copy(j, line(j, 3, 0, part), g2s.at[j, 2 + k], g2r.at[j, 2 + k], sibling).wait_recv()
            own(j, 3)
        for load in loads:
            load.wait()
        for j in range(3):
            relay(j, 1)
            add(j, plane(j, 0), core)
        for j in range(3):
            relay(j, 2)
        forwarded(0)
        adds(0, rest)
        add_dense(2)
        forwarded(1, (0,))
        forwarded(2, (0,))
        add_dense(0)
        for j in range(3):
            relay(j, 3)
        adds(1, core)
        adds(2, core)

        def last(n):
            for j in range(3):
                for k, part in enumerate((lower, upper)):
                    copy(j, line(j, n, 3, part), g3s.at[j, n, 2 + k], g3r.at[j, n, 2 + k], sibling).wait_recv()
                forward(j, n, 3)

        last(0)
        last(1)
        forwarded(1, (1, 2, 3))
        adds(1, rest)
        last(2)
        forwarded(2, (1, 2, 3))
        adds(2, rest)
        def glu(v):
            g, u = v[:, :304], v[:, 304:]
            return (g / (1.0 + jnp.exp(-g)) * u).astype(BF16)

        add_lines(3, core, (0, 1))
        forwarded(3, (0, 1))
        add_lines(3, rest, (0, 1))
        forwarded(3, (2,))
        add_dense(1)
        hd[...] = glu(acc_d[...])
        trade.start()
        last(3)
        add_lines(3, core, (2, 3))
        forwarded(3, (3,))
        add_lines(3, rest, (2, 3))

        e = lax.axis_index("expert")
        lanes = lax.broadcasted_iota(jnp.int32, (256, 128), 1)
        pick = jnp.where(lanes == e, 32.0, 0.0) + jnp.where(lanes == e + 8, 1.0, 0.0)
        for x in range(4):
            he[x] = glu(acc[x].reshape(256, 608)).reshape(4, 4, 16, 304)
            trades[x].start()
        for x in range(4):
            pieces = x2[core, x, :, :, :, WIDTHS[2] :].reshape(256, 128).astype(F32)
            weight[x] = (jnp.sum(pieces * pick, axis=1, keepdims=True) * (1.0 / 1024.0)).reshape(4, 4, 16, 1)
        for lend in lends:
            lend.wait_recv()
        settle()

    def reduce(z0, z1, z2, q0, q1, q2):
        zs, dense = (z0, z1, z2), (q0, q1, q2)
        half1, full1, half2, full2, last_in = (a0, a1, a2), (b0, b1, b2), (c0, c1, c2), (d0, d1, d2), (t0, t1, t2)
        staged = (u0, u1, u2)

        def where(j, step):
            b1, b2, b3 = REDUCE[j]
            return at({b1: lax.rem(pos[b1] + step, 4), b2: ALL, b3: ALL})

        def produce(j, step):
            cols = slice(STARTS[j], STARTS[j] + WIDTHS[j])
            idx = where(j, step)
            part = dot(heb[idx].reshape(256, 608), down_e[:, cols]) * weight[idx].reshape(256, 1)
            zs[j][idx] = part.astype(BF16).reshape(4, 4, 16, WIDTHS[j])

        def produce_dense(j, step):
            idx = where(j, step)
            axis = REDUCE[j][0]
            places = []
            if axis == 0 and step == 0:
                places = [((idx[0], ALL, pos[2]), (0, ALL))]
            elif axis == 1:
                places = [((dense_x[k], idx[1], pos[2]), (k, idx[1])) for k in range(2)]
            elif axis == 2 and step == 0:
                places = [((dense_x[k], ALL, pos[2]), (k, ALL)) for k in range(2)]
            elif axis == 0 and step % 2:

                @pl.when(idx[0] == dense_x[1])
                def _():
                    spot = (idx[0], ALL, pos[2])
                    zs[j][spot] = (zs[j][spot].astype(F32) + dense[j][1]).astype(BF16)

            for spot, src in places:
                zs[j][spot] = (zs[j][spot].astype(F32) + dense[j][src]).astype(BF16)

        def gain(j, idx, *others):
            total = zs[j][idx].astype(F32)
            for other in others:
                total = total + other[...].astype(F32)
            zs[j][idx] = total.astype(BF16)

        def row(j, step, r, part=ALL):
            b1, b2, b3 = REDUCE[j]
            return at({b1: lax.rem(pos[b1] + step, 4), b2: lax.rem(pos[b2] + r, 4), b3: part})

        def halves(j, step, r, axis, bufs, ss, rr):
            for k, (part, d) in enumerate(((lower, 1), (upper, 3))):
                go(remote(zs[j].at[row(j, step, r, part)], bufs.at[k], ss.at[k], rr.at[k], device(moved(pos, axis, d), core)))

        def whole(j, step, r, axis, k, bufs, fulls, ss, rr):
            part, d = ((lower, 1), (upper, 3))[k]
            remote(bufs.at[k], bufs.at[k], ss.at[k], rr.at[k], sibling).wait_recv()
            gain(j, row(j, step, r, part), bufs.at[k])
            go(remote(zs[j].at[row(j, step, r)], fulls.at[k], ss.at[2 + k], rr.at[2 + k], device(moved(pos, axis, d), core)))

        def close(j, r, fulls, ss, rr):
            for k in range(2):
                remote(fulls.at[k], fulls.at[k], ss.at[2 + k], rr.at[2 + k], sibling).wait_recv()
            gain(j, row(j, 0, r), fulls.at[0], fulls.at[1])

        def outer(j, n):
            return (half1[j].at[n], full1[j].at[n], s1.at[j, n], r1.at[j, n])

        def inner(j):
            return (half2[j], full2[j], s2.at[j], r2.at[j])

        order = (2, 1, 3, 0)
        def begin(j, i):
            bufs, _, ss, rr = outer(j, i)
            halves(j, 2, order[i], REDUCE[j][0], bufs, ss, rr)

        def go_on(j, i, k):
            bufs, fulls, ss, rr = outer(j, i)
            whole(j, order[1 + k], order[i], REDUCE[j][0], k, bufs, fulls, ss, rr)

        trade.wait_recv()
        hdb[...] = jnp.concatenate([hd[...], hd_in[...]], axis=1)
        for j in range(3):
            part = dot(hdb[...], down_d[:, STARTS[j] : STARTS[j] + WIDTHS[j]])
            dense[j][...] = part.reshape(2, 4, 16, WIDTHS[j])
        for x in range(4):
            trades[x].wait_recv()
            heb[x] = jnp.concatenate([he[x].reshape(256, 304), he_in[x].reshape(256, 304)], axis=1).reshape(4, 4, 16, 608)
        for j in range(3):
            produce(j, 2)
            produce_dense(j, 2)
            begin(j, 0)
        def next_line(i):
            for j in range(3):
                for k in range(2):
                    go_on(j, i, k)

        for k in range(2):
            for j in range(3):
                produce(j, order[1 + k])
                produce_dense(j, order[1 + k])
                begin(j, 1 + k)
        next_line(0)
        for j in range(3):
            begin(j, 3)
        next_line(1)
        for j in range(3):
            produce(j, 0)
            produce_dense(j, 0)
        for i, r in enumerate(order):
            if i in (1, 2):
                next_line(i + 1)
            for j in range(3):
                _, fulls, ss, rr = outer(j, i)
                close(j, r, fulls, ss, rr)
                bufs, fulls, ss, rr = inner(j)
                if r == 2:
                    halves(j, 0, r, REDUCE[j][1], bufs, ss, rr)
                elif r:
                    whole(j, 0, r, REDUCE[j][1], i - 1, bufs, fulls, ss, rr)
        for j in range(3):
            _, fulls, ss, rr = inner(j)
            close(j, 0, fulls, ss, rr)
            for k, d in enumerate((*STEPS, 0)):
                there = moved(pos, REDUCE[j][2], d)
                rows = zs[j][there].astype(F32)
                for c in range(2):
                    staged[j][k, c] = rows[c * 8 : c * 8 + 8].astype(BF16)
                for i, c in enumerate((core, rest)):
                    if d or i:
                        src, dst = staged[j].at[k, c], last_in[j].at[k, core]
                        go(remote(src, dst, s3.at[j, k, i], r3.at[j, k, core], device(there, c)))
        for j in range(3):
            for i, half in enumerate((core, rest)):
                total = staged[j][3, core].astype(F32) if i == 0 else 0.0
                for k in range(3 + i):
                    got = last_in[j].at[k, half]
                    remote(got, got, s3.at[j, k, i], r3.at[j, k, half], sibling).wait_recv()
                    total = total + got[...].astype(F32)
                cols = pl.ds(pl.multiple_of(half * HALF + STARTS[j], 128), WIDTHS[j])
                out[:, cols] = (tok[:, cols].astype(F32) + total).astype(BF16)
        for copy in (*trades, trade):
            copy.wait_send()
        settle()

    wide = (608, tok.shape[1])
    pl.run_scoped(
        gather,
        pltpu.VMEM(wide, BF16),
        pltpu.VMEM(wide, BF16),
        pltpu.VMEM((4, 4, 4, 16, 608), F32),
        pltpu.VMEM((128, 608), F32),
    )
    pl.run_scoped(
        reduce,
        *(pltpu.VMEM((4, 4, 4, 16, w), BF16) for w in WIDTHS),
        *(pltpu.VMEM((2, 4, 16, w), F32) for w in WIDTHS),
    )


def per_device(
    tokens, route_ids, route_gain, norm_gain, dense_gate, dense_up, dense_down, expert_gate, expert_up, expert_down
):
    vmem = pl.BlockSpec(memory_space=pltpu.VMEM)
    hbm = pl.BlockSpec(memory_space=pl.ANY)
    dma = pltpu.SemaphoreType.DMA
    d, f = dense_gate.shape

    def sized(*lead):
        return [pltpu.VMEM((*lead, w), BF16) for w in WIDTHS]

    gathered = [pltpu.VMEM((2, 4, 4, 4, 16, w + (128 if j == 2 else 0)), BF16) for j, w in enumerate(WIDTHS)]
    return pl.pallas_call(
        block_kernel,
        out_shape=jax.ShapeDtypeStruct(tokens.shape, BF16),
        in_specs=[vmem] * 4 + [hbm] * 6,
        out_specs=vmem,
        scratch_shapes=gathered
        + [pltpu.VMEM((2, 8, HALF + 128), BF16), pltpu.VMEM((8, HALF + 128), BF16)]
        + [pltpu.VMEM((3, 2, 8, x.shape[-1]), BF16) for x in gathered]
        + [pltpu.VMEM((2 * f, HALF), BF16)] * 2
        + [pltpu.VMEM((4, 4, 4, 16, f), BF16)] * 2
        + [pltpu.VMEM((4, 4, 4, 16, 2 * f), BF16)]
        + [pltpu.VMEM((128, f), BF16)] * 2
        + [pltpu.VMEM((128, 2 * f), BF16), pltpu.VMEM((4, 4, 4, 16, 1), F32)]
        + sized(4, 2, 2, 16)
        + sized(4, 2, 4, 16)
        + sized(2, 2, 16)
        + sized(2, 4, 16)
        + sized(4, 2, 8)
        + sized(4, 2, 8)
        + [dma((6,)), dma((2,)), dma((2,)), dma, dma]
        + [dma((3, 3, 2))] * 2
        + [dma((3, 4))] * 2
        + [dma((3, 4, 4))] * 4
        + [dma((4,)), dma((4,)), dma, dma]
        + [dma((3, 4, 4))] * 2
        + [dma((3, 4))] * 2
        + [dma((3, 4, 2))] * 2,
        compiler_params=pltpu.CompilerParams(
            collective_id=0, has_side_effects=True, vmem_limit_bytes=60 * 1024 * 1024
        ),
        name="gather_experts_sum",
    )(
        tokens, route_ids.T, route_gain.T, norm_gain.reshape(1, d),
        expert_gate.reshape(d, f).T, expert_up.reshape(d, f).T, dense_gate.T, dense_up.T,
        expert_down.reshape(f, d), dense_down,
    )


def solution(mesh):
    rows = P(("expert", "tensor"), None)
    return jax.shard_map(
        per_device,
        mesh=mesh,
        in_specs=(
            rows, rows, rows, P(),
            P(None, "tensor"), P(None, "tensor"), P("tensor", None),
            P("expert", None, "tensor"), P("expert", None, "tensor"), P("expert", "tensor", None),
        ),
        out_specs=rows,
        check_vma=False,
    )
```
